32 devices in a mesh: dom: 2 (over y), dp: 16 (over z, x, core).
Axes of the slice: x: 2, y: 2, z: 4, core: 2. Of those that a mesh axis runs over, the one named last changes fastest.
Arguments:
- positions: float32 [128, 32768], P('dom', 'dp'), may hold values from -6 to 6
- ancestors: int32 [128], P('dom'), may hold values from 0 to 127
- block_choice: int32 [16, 16], replicated, may hold values from 0 to 15
- tile_slot: int32 [256, 8], P('dp'), may hold values from 0 to 15, all different within a row
- design: bfloat16 [32768, 1024], P('dp'), may hold values from -0.1875 to 0.1875
- labels: int32 [32768], P('dp'), may hold values 0 or 1
- row_section: int32 [32768], P('dp'), may hold values from 0 to 4
Outputs:
- advanced: float32 [128, 32768], P('dom', 'dp')
- mean_loglik: float32 [128], P('dom')
The draws below stay inside these ranges and needn't reach their ends.
Inputs may be any that keep to these rules, and one draw needn't show every extreme that they name: Each row of tile_slot names 8 different owners.
All inputs are finite; a program needn't handle non-finite values. No bound on the sum of `labels` on one device may be relied on, other than what follows from the above.
Results may differ from the reference program's by a relative error of at most 0.00048.
Values may be sent and summed in bfloat16 or wider, within the bound.
A program may use at most 64 MiB of HBM per device.

```python
import jax
import jax.numpy as jnp
from jax import lax

F = 32768
TILE = 128
K = 8
SECTIONS = 5
CURRENT = 2
RB_DEV = 16
P_SIZE = 128
ROWS = 32768
BLK_OWN = 16
N_DP = 16


def place_ends(entries, own_key, low, high):
    dims = entries.shape
    index_at = [jax.random.randint(jax.random.fold_in(own_key, axis), (), 0, dims[axis]) for axis in range(len(dims))]
    entries = entries.at[tuple(index_at)].set(low)
    longest = dims.index(max(dims))
    index_at[longest] = (index_at[longest] + 1) % dims[longest]
    return entries.at[tuple(index_at)].set(high)


def level_of(stream_key, shape, cuts, least, top_value):
    factor_of, own = 1.0, jax.random.fold_in(stream_key, 6)
    for position, blocks in cuts:
        draws = jnp.exp(jax.random.uniform(jax.random.fold_in(own, position), (blocks,), jnp.float32, least / len(cuts), top_value / len(cuts)))
        factor_of = factor_of * jnp.repeat(draws, shape[position] // blocks).reshape([-1 if axis == position else 1 for axis in range(len(shape))])
    return factor_of


def different_ones(rng, rows, count, top, lift):
    order = jax.random.permutation(jax.random.fold_in(rng, 1), count)
    favour = order
    for power in range(3):
        favour = favour * favour // count
    favour = favour * lift // count
    lots = jax.random.randint(jax.random.fold_in(rng, 2), (rows, count), 0, 4096) + favour
    holders = jax.random.permutation(jax.random.fold_in(rng, 3), rows)[jnp.arange(count) % rows]
    lots = jnp.where(jnp.arange(rows)[:, None] == holders[None, :], 1 << 14, lots)
    priority = lots * count + jnp.arange(count)
    return lax.top_k(priority.astype(jnp.int32), top)[1].astype(jnp.int32)


def normal_values(stream_key, dims, width, bound, split=(), held_as=jnp.bfloat16):
    array = jax.random.normal(stream_key, dims, jnp.float32) * width
    if len(split) > 0:
        array = level_of(stream_key, dims, split, -0.22, 0.18) * array
    return jnp.clip(array, min=-bound, max=bound).astype(held_as)


def setup_inputs(seed: int = 0) -> dict:
    keys = jax.random.split(jax.random.key(seed), 8)
    positions = normal_values(keys[0], (P_SIZE, F), 1.0, 6.0, ((0, 2), (1, 16)), jnp.float32)
    ancestors = place_ends(jax.random.randint(keys[1], (P_SIZE,), 0, P_SIZE), jax.random.fold_in(keys[1], 1), 0, P_SIZE - 1).astype(jnp.int32)
    block_choice = place_ends(jax.random.randint(keys[2], (N_DP, N_DP), 0, BLK_OWN), jax.random.fold_in(keys[2], 1), 0, BLK_OWN - 1).astype(jnp.int32)
    tile_slot = different_ones(keys[3], (RB_DEV * N_DP), N_DP, K, 4096)
    design = normal_values(keys[4], (ROWS, K * TILE), (K * TILE) ** -0.5, 0.1875, ((0, 16),))
    labels = place_ends((jax.random.randint(keys[5], (ROWS,), 0, 2) < 1).astype(jnp.int32), jax.random.fold_in(keys[5], 1), 0, 1)
    row_section = place_ends(jax.random.randint(keys[6], (ROWS,), 0, SECTIONS), jax.random.fold_in(keys[6], 1), 0, SECTIONS - 1).astype(jnp.int32)
    return dict(positions=positions, ancestors=ancestors, block_choice=block_choice, tile_slot=tile_slot, design=design, labels=labels, row_section=row_section)


step_size = 1.0
prior_precision = 0.05


def tile_logits(narrow, design_tiles, blocks):
    weights = jnp.take(narrow, blocks, axis=1).astype(jnp.float32)
    return jnp.einsum('bikc,pbkc->bpi', design_tiles.astype(jnp.float32), weights)


def reference(positions, ancestors, block_choice, tile_slot, design, labels, row_section):
    blocks_owned = F // (TILE * N_DP)
    blocks_dev = tile_slot.shape[0] // N_DP
    particle_count = positions.shape[0]
    resampled = jnp.take(positions, ancestors, axis=0)
    design_all = design.reshape(N_DP, blocks_dev, TILE, K, TILE)
    slots = tile_slot.reshape(N_DP, blocks_dev, K)
    owner_pick = block_choice[jnp.arange(N_DP)[:, None, None], slots]
    feature_blocks = (slots * blocks_owned + owner_pick).astype(jnp.int32)
    targets = labels.reshape(N_DP, blocks_dev, 1, TILE).astype(jnp.float32)
    sections = row_section.reshape(N_DP, blocks_dev, 1, TILE)
    narrow = resampled.astype(jnp.bfloat16).reshape(particle_count, F // TILE, TILE)

    def add_gradient(total, packed):
        design_tiles, blocks, target_rows, section_rows = packed
        logits = tile_logits(narrow, design_tiles, blocks)
        residual = jnp.where(section_rows <= CURRENT, target_rows - jax.nn.sigmoid(logits), 0.0).astype(jnp.bfloat16)
        per_tile = jnp.einsum('bpi,bikc->pbkc', residual.astype(jnp.float32), design_tiles.astype(jnp.float32))
        return total.at[:, blocks].add(per_tile), None

    gradient_start = jnp.zeros((particle_count, F // TILE, TILE), jnp.float32)
    gradient, unused = lax.scan(add_gradient, gradient_start, (design_all, feature_blocks, targets, sections))
    advanced = resampled + step_size * (gradient.reshape(particle_count, F) - prior_precision * resampled)
    narrow_new = advanced.astype(jnp.bfloat16).reshape(particle_count, F // TILE, TILE)

    def add_likelihood(carry, packed):
        totals, counted = carry
        design_tiles, blocks, target_rows, section_rows = packed
        logits = tile_logits(narrow_new, design_tiles, blocks)
        chosen = section_rows == CURRENT + 1
        loglik = jnp.where(chosen, target_rows * logits - jax.nn.softplus(logits), 0.0)
        return (totals + jnp.sum(loglik, axis=(0, 2)), counted + jnp.sum(chosen.astype(jnp.float32))), None

    start = (jnp.zeros((particle_count,), jnp.float32), jnp.zeros((), jnp.float32))
    (totals, counted), unused = lax.scan(add_likelihood, start, (design_all, feature_blocks, targets, sections))
    return advanced, totals / jnp.maximum(counted, 1.0)
```

```python
import functools

import jax
import jax.numpy as jnp
from jax import lax
from jax.experimental import pallas as pl
from jax.experimental.pallas import tpu as pltpu
from jax.sharding import PartitionSpec as P

TILE = 128
CURRENT = 2
STEP_SIZE = 1.0
PRIOR_PRECISION = 0.05
MESH = pl.DeviceIdType.MESH
F32, BF16 = jnp.float32, jnp.bfloat16


def round_kernel(
    groups,
    width,
    choice,
    slots,
    inverse,
    positions,
    ancestors,
    design_hbm,
    labels,
    sections,
    advanced,
    mean_out,
    design,
    narrow,
    picked,
    picked_all,
    lineage,
    resampled,
    outgoing,
    fetched,
    terms,
    sums,
    incoming,
    outgoing_new,
    fetched_new,
    totals_own,
    totals_all,
    design_sem,
    dom_send,
    dom_recv,
    pos_send,
    pos_recv,
    out_send,
    out_recv,
    grad_send,
    grad_recv,
    new_send,
    new_recv,
    tot_send,
    tot_recv,
):
    me, group = lax.axis_index("dp"), lax.axis_index("dom")
    particles = positions.shape[0]
    blocks_owned = positions.shape[1] // TILE
    blocks_dev, per_block = slots.shape

    def to_dp(source, target, sends, receives, device):
        return pltpu.make_async_remote_copy(
            src_ref=source,
            dst_ref=target.at[me],
            send_sem=sends.at[device],
            recv_sem=receives.at[me],
            device_id=(group, device),
            device_id_type=MESH,
        )

    def from_dp(source, target, sends, receives, device):
        return pltpu.make_async_remote_copy(
            src_ref=source,
            dst_ref=target.at[device],
            send_sem=sends.at[device],
            recv_sem=receives.at[device],
            device_id=(group, device),
            device_id_type=MESH,
        )

    def others(body):
        def step(offset, carry):
            body(lax.rem(me + offset, width))
            return carry

        lax.fori_loop(1, width, step, 0)

    barrier = pltpu.get_barrier_semaphore()

    def greet(device):
        pl.semaphore_signal(barrier, inc=1, device_id=(group, device), device_id_type=MESH)

    others(greet)
    for offset in range(1, groups):
        pl.semaphore_signal(
            barrier, inc=1, device_id=(lax.rem(group + offset, groups), me), device_id_type=MESH
        )
    design_copy = pltpu.make_async_copy(design_hbm, design, design_sem)
    design_copy.start()

    for block in range(blocks_owned):
        narrow[block] = positions[:, block * TILE : (block + 1) * TILE].astype(BF16)

    def pick(device, carry):
        value = narrow[choice[device, me]]
        picked[device] = value
        picked_all[group, device] = value
        return carry

    lax.fori_loop(0, width, pick, 0)
    origin = lax.broadcasted_iota(jnp.int32, (groups * particles, particles), 0)
    hot = (origin == ancestors[...]).astype(F32).T.astype(BF16)
    pl.semaphore_wait(barrier, width + groups - 2)

    def dom_copy(device, offset, incoming_side):
        sign = groups - offset if incoming_side else offset
        peer = lax.rem(group + sign, groups)
        return pltpu.make_async_remote_copy(
            src_ref=picked.at[device],
            dst_ref=picked_all.at[peer if incoming_side else group, device],
            send_sem=dom_send.at[offset - 1, device],
            recv_sem=dom_recv.at[offset - 1, device],
            device_id=(peer, me),
            device_id_type=MESH,
        )

    def position_copy(offset, incoming_side):
        sign = groups - offset if incoming_side else offset
        peer = lax.rem(group + sign, groups)
        return pltpu.make_async_remote_copy(
            src_ref=positions,
            dst_ref=lineage.at[peer if incoming_side else group],
            send_sem=pos_send.at[offset - 1],
            recv_sem=pos_recv.at[offset - 1],
            device_id=(peer, me),
            device_id_type=MESH,
        )

    def send_picked(device):
        for offset in range(1, groups):
            dom_copy(device, offset, False).start()

    others(send_picked)
    send_picked(me)
    for offset in range(1, groups):
        position_copy(offset, False).start()

    def resample(device):
        for offset in range(1, groups):
            dom_copy(device, offset, True).wait_recv()
        rows = picked_all[:, device].reshape(groups * particles, TILE)
        return jnp.dot(hot, rows, preferred_element_type=F32).astype(BF16)

    def send_resampled(device):
        outgoing[device] = resample(device)
        to_dp(outgoing.at[device], fetched, out_send, out_recv, device).start()

    others(send_resampled)
    fetched[me] = resample(me)
    terms[blocks_dev * per_block] = jnp.zeros((particles, TILE), F32)
    design_copy.wait()
    others(lambda device: from_dp(outgoing.at[device], fetched, out_send, out_recv, device).wait_recv())

    def logits_of(source, row_block):
        weights = jnp.concatenate(
            [source[slots[row_block, place]] for place in range(per_block)], axis=1
        )
        tiles = design[pl.ds(pl.multiple_of(row_block * TILE, TILE), TILE), :]
        logits = lax.dot_general(
            weights, tiles, (((1,), (1,)), ((), ())), preferred_element_type=F32
        )
        target = labels[pl.ds(row_block, 1), :].astype(F32)
        section = sections[pl.ds(row_block, 1), :]
        return tiles, logits, target, section

    def gradient_terms(row_block, carry):
        tiles, logits, target, section = logits_of(fetched, row_block)
        residual = jnp.where(section <= CURRENT, target - jax.nn.sigmoid(logits), 0.0).astype(BF16)
        product = jnp.dot(residual, tiles, preferred_element_type=F32)
        for place in range(per_block):
            terms[row_block * per_block + place] = product[:, place * TILE : (place + 1) * TILE]
        return carry

    lax.fori_loop(0, blocks_dev, gradient_terms, 0, unroll=4)

    def summed(device):
        total = terms[inverse[device, 0]]
        for row_block in range(1, blocks_dev):
            total = total + terms[inverse[device, row_block]]
        return total

    def send_sum(device):
        sums[device] = summed(device)
        to_dp(sums.at[device], incoming, grad_send, grad_recv, device).start()

    others(send_sum)
    incoming[me] = summed(me)

    lineage[group] = positions[...]
    for offset in range(1, groups):
        position_copy(offset, True).wait_recv()
    for block in range(blocks_owned):
        span = slice(block * TILE, (block + 1) * TILE)
        rows = lineage[:, :, span].reshape(groups * particles, TILE)
        high = rows.astype(BF16)
        low = (rows - high.astype(F32)).astype(BF16)
        resampled[block] = jnp.dot(hot, high, preferred_element_type=F32) + jnp.dot(
            hot, low, preferred_element_type=F32
        )

    others(lambda device: from_dp(sums.at[device], incoming, grad_send, grad_recv, device).wait_recv())
    for block in range(blocks_owned):
        gradient = jnp.zeros((particles, TILE), F32)
        for device in range(width):
            mine = (choice[device, me] == block).astype(F32)
            gradient = gradient + mine * incoming[device]
        kept = resampled[block]
        moved = kept + STEP_SIZE * (gradient - PRIOR_PRECISION * kept)
        advanced[:, block * TILE : (block + 1) * TILE] = moved
        narrow[block] = moved.astype(BF16)

    def send_new(device):
        outgoing_new[device] = narrow[choice[device, me]]
        to_dp(outgoing_new.at[device], fetched_new, new_send, new_recv, device).start()

    others(send_new)
    fetched_new[me] = narrow[choice[me, me]]
    others(
        lambda device: from_dp(
            outgoing_new.at[device], fetched_new, new_send, new_recv, device
        ).wait_recv()
    )

    def likelihood(row_block, carry):
        total, counted = carry
        _, logits, target, section = logits_of(fetched_new, row_block)
        chosen = section == CURRENT + 1
        softplus = jnp.maximum(logits, 0.0) + jnp.log(1.0 + jnp.exp(-jnp.abs(logits)))
        return (
            total + jnp.where(chosen, target * logits - softplus, 0.0),
            counted + chosen.astype(F32),
        )

    total, counted = lax.fori_loop(
        0,
        blocks_dev,
        likelihood,
        (jnp.zeros((particles, TILE), F32), jnp.zeros((1, TILE), F32)),
        unroll=4,
    )
    both = jnp.concatenate([total, jnp.broadcast_to(counted, (particles, TILE))], axis=0)
    row = jnp.sum(both.T, axis=0, keepdims=True)
    row = jnp.broadcast_to(row, totals_own.shape)
    totals_own[...] = row
    totals_all[me] = row
    others(lambda device: to_dp(totals_own, totals_all, tot_send, tot_recv, device).start())
    others(lambda device: from_dp(totals_own, totals_all, tot_send, tot_recv, device).wait_recv())
    final = jnp.sum(totals_all[...], axis=0)
    mean_out[...] = final[:1, :particles] / jnp.maximum(final[:1, particles:], 1.0)

    def wait_sends(device):
        to_dp(outgoing.at[device], fetched, out_send, out_recv, device).wait_send()
        to_dp(sums.at[device], incoming, grad_send, grad_recv, device).wait_send()
        to_dp(outgoing_new.at[device], fetched_new, new_send, new_recv, device).wait_send()
        to_dp(totals_own, totals_all, tot_send, tot_recv, device).wait_send()

    others(wait_sends)

    def wait_dom(device, carry):
        for offset in range(1, groups):
            dom_copy(device, offset, False).wait_send()
        return carry

    lax.fori_loop(0, width, wait_dom, 0)
    for offset in range(1, groups):
        position_copy(offset, False).wait_send()


def shards(positions, ancestors, block_choice, tile_slot, design, labels, row_section):
    width, groups = lax.axis_size("dp"), lax.axis_size("dom")
    particles, features = positions.shape
    blocks_owned = features // TILE
    blocks_dev, per_block = tile_slot.shape
    tiles = blocks_dev * per_block
    numbers = jnp.arange(tiles, dtype=jnp.int32).reshape(1, blocks_dev, per_block)
    owners = jnp.arange(width, dtype=jnp.int32)[:, None, None]
    inverse = jnp.min(jnp.where(tile_slot[None] == owners, numbers, tiles), axis=2)

    smem = pl.BlockSpec(memory_space=pltpu.SMEM)
    vmem = pl.BlockSpec(memory_space=pltpu.VMEM)
    block = (particles, TILE)
    dma = pltpu.SemaphoreType.DMA
    advanced, mean = pl.pallas_call(
        functools.partial(round_kernel, groups, width),
        out_shape=(
            jax.ShapeDtypeStruct((particles, features), F32),
            jax.ShapeDtypeStruct((1, particles), F32),
        ),
        in_specs=[smem, smem, smem, vmem, vmem, pl.BlockSpec(memory_space=pl.ANY), vmem, vmem],
        out_specs=(vmem, vmem),
        scratch_shapes=[
            pltpu.VMEM(design.shape, BF16),
            pltpu.VMEM((blocks_owned, *block), BF16),
            pltpu.VMEM((width, *block), BF16),
            pltpu.VMEM((groups, width, *block), BF16),
            pltpu.VMEM((groups, particles, features), F32),
            pltpu.VMEM((blocks_owned, *block), F32),
            pltpu.VMEM((width, *block), BF16),
            pltpu.VMEM((width, *block), BF16),
            pltpu.VMEM((tiles + 1, *block), F32),
            pltpu.VMEM((width, *block), F32),
            pltpu.VMEM((width, *block), F32),
            pltpu.VMEM((width, *block), BF16),
            pltpu.VMEM((width, *block), BF16),
            pltpu.VMEM((8, 2 * particles), F32),
            pltpu.VMEM((width, 8, 2 * particles), F32),
            dma,
            dma((max(groups - 1, 1), width)),
            dma((max(groups - 1, 1), width)),
            dma((max(groups - 1, 1),)),
            dma((max(groups - 1, 1),)),
            dma((width,)),
            dma((width,)),
            dma((width,)),
            dma((width,)),
            dma((width,)),
            dma((width,)),
            dma((width,)),
            dma((width,)),
        ],
        compiler_params=pltpu.CompilerParams(
            collective_id=0, has_side_effects=True, vmem_limit_bytes=48 << 20
        ),
        name="smc_round",
    )(
        block_choice,
        tile_slot,
        inverse,
        positions,
        ancestors.reshape(1, particles),
        design,
        labels.reshape(blocks_dev, TILE),
        row_section.reshape(blocks_dev, TILE),
    )
    return advanced, mean.reshape(particles)


def solution(mesh):
    return jax.shard_map(
        shards,
        mesh=mesh,
        in_specs=(P("dom", "dp"), P("dom"), P(), P("dp", None), P("dp", None), P("dp"), P("dp")),
        out_specs=(P("dom", "dp"), P("dom")),
        check_vma=False,
    )
```

```python
import functools

import jax
import jax.numpy as jnp
from jax import lax
from jax.experimental import pallas as pl
from jax.experimental.pallas import tpu as pltpu
from jax.sharding import PartitionSpec as P

TILE = 128
CURRENT = 2
STEP_SIZE = 1.0
PRIOR_PRECISION = 0.05
ARRIVALS = 4
TERM = jnp.float32
MESH = pl.DeviceIdType.MESH
F32, BF16 = jnp.float32, jnp.bfloat16


def round_kernel(
    groups,
    width,
    choice_in,
    slots_in,
    positions_in,
    ancestors_in,
    design_in,
    labels_in,
    sections_in,
    advanced_out,
    mean_out,
    choice,
    slots,
    slots_wide,
    inverse_wide,
    inverse,
    positions,
    ancestors,
    labels,
    sections,
    advanced,
    gradient,
    design,
    narrow,
    picked,
    picked_all,
    lineage,
    resampled,
    outgoing,
    fetched,
    terms,
    sums,
    incoming,
    outgoing_new,
    fetched_new,
    totals_own,
    totals_all,
    load_sem,
    inverse_sem,
    store_sem,
    dom_send,
    dom_recv,
    pos_send,
    pos_recv,
    out_send,
    out_recv,
    grad_send,
    grad_recv,
    new_send,
    new_recv,
    tot_send,
    tot_recv,
):
    me, group = lax.axis_index("dp"), lax.axis_index("dom")
    particles = positions.shape[0]
    blocks_owned = positions.shape[1] // TILE
    per_block, blocks_dev = slots.shape
    loads = [
        pltpu.make_async_copy(source, target, load_sem.at[number])
        for number, (source, target) in enumerate(
            (
                (positions_in, positions),
                (choice_in, choice),
                (slots_in, slots_wide),
                (ancestors_in, ancestors),
                (slots_in, slots),
                (labels_in, labels),
                (sections_in, sections),
                (design_in, design),
            )
        )
    ]
    for load in loads:
        load.start()

    def to_dp(source, target, sends, receives, device):
        return pltpu.make_async_remote_copy(
            src_ref=source,
            dst_ref=target.at[me],
            send_sem=sends.at[device],
            recv_sem=receives.at[me],
            device_id=(group, device),
            device_id_type=MESH,
        )

    def from_dp(source, target, sends, receives, device):
        return pltpu.make_async_remote_copy(
            src_ref=source,
            dst_ref=target.at[device],
            send_sem=sends.at[device],
            recv_sem=receives.at[device],
            device_id=(group, device),
            device_id_type=MESH,
        )

    def others(body):
        def step(offset, carry):
            body(lax.rem(me + offset, width))
            return carry

        lax.fori_loop(1, width, step, 0)

    barrier = pltpu.get_barrier_semaphore()

    def greet(device):
        pl.semaphore_signal(barrier, inc=1, device_id=(group, device), device_id_type=MESH)

    others(greet)
    for offset in range(1, groups):
        pl.semaphore_signal(
            barrier, inc=1, device_id=(lax.rem(group + offset, groups), me), device_id_type=MESH
        )
    for load in loads[:4]:
        load.wait()
    for block in range(blocks_owned):
        narrow[block] = positions[:, block * TILE : (block + 1) * TILE].astype(BF16)

    def pick(device, carry):
        value = narrow[choice[device, me]]
        picked[device] = value
        picked_all[group, device] = value
        return carry

    lax.fori_loop(0, width, pick, 0)
    origin = lax.broadcasted_iota(jnp.int32, (groups * particles, particles), 0)
    hot = (origin == ancestors[...]).astype(F32).T.astype(BF16)
    tiles_dev = blocks_dev * per_block
    owner = lax.broadcasted_iota(jnp.int32, (width, blocks_dev), 0)
    first = lax.broadcasted_iota(jnp.int32, (width, blocks_dev), 1) * per_block
    found = jnp.full((width, blocks_dev), tiles_dev, jnp.int32)
    for place in range(per_block):
        found = jnp.where(slots_wide[place : place + 1, :] == owner, first + place, found)
    inverse_wide[...] = found
    inverse_copy = pltpu.make_async_copy(inverse_wide, inverse, inverse_sem)
    inverse_copy.start()
    pl.semaphore_wait(barrier, width + groups - 2)

    def dom_copy(device, offset, incoming_side):
        sign = groups - offset if incoming_side else offset
        peer = lax.rem(group + sign, groups)
        return pltpu.make_async_remote_copy(
            src_ref=picked.at[device],
            dst_ref=picked_all.at[peer if incoming_side else group, device],
            send_sem=dom_send.at[offset - 1, device],
            recv_sem=dom_recv.at[offset - 1, device],
            device_id=(peer, me),
            device_id_type=MESH,
        )

    def position_copy(offset, incoming_side):
        sign = groups - offset if incoming_side else offset
        peer = lax.rem(group + sign, groups)
        return pltpu.make_async_remote_copy(
            src_ref=positions,
            dst_ref=lineage.at[peer if incoming_side else group],
            send_sem=pos_send.at[offset - 1],
            recv_sem=pos_recv.at[offset - 1],
            device_id=(peer, me),
            device_id_type=MESH,
        )

    def send_picked(device):
        for offset in range(1, groups):
            dom_copy(device, offset, False).start()

    others(send_picked)
    send_picked(me)
    for offset in range(1, groups):
        position_copy(offset, False).start()

    def resample(device):
        for offset in range(1, groups):
            dom_copy(device, offset, True).wait_recv()
        rows = picked_all[:, device].reshape(groups * particles, TILE)
        return jnp.dot(hot, rows, preferred_element_type=F32).astype(BF16)

    def send_resampled(device):
        outgoing[device] = resample(device)
        to_dp(outgoing.at[device], fetched, out_send, out_recv, device).start()

    others(send_resampled)
    fetched[me] = resample(me)
    terms[tiles_dev] = jnp.zeros((particles, TILE), F32)
    for load in loads[4:]:
        load.wait()
    inverse_copy.wait()
    others(lambda device: from_dp(outgoing.at[device], fetched, out_send, out_recv, device).wait_recv())

    def logits_of(source, row_block):
        weights = jnp.concatenate(
            [source[slots[place, row_block]] for place in range(per_block)], axis=1
        )
        tiles = design[pl.ds(pl.multiple_of(row_block * TILE, TILE), TILE), :]
        logits = lax.dot_general(
            weights, tiles, (((1,), (1,)), ((), ())), preferred_element_type=F32
        )
        target = labels[pl.ds(row_block, 1), :].astype(F32)
        section = sections[pl.ds(row_block, 1), :]
        return tiles, logits, target, section

    def gradient_terms(row_block, carry):
        tiles, logits, target, section = logits_of(fetched, row_block)
        residual = jnp.where(section <= CURRENT, target - jax.nn.sigmoid(logits), 0.0).astype(BF16)
        product = jnp.dot(residual, tiles, preferred_element_type=F32)
        for place in range(per_block):
            terms[row_block * per_block + place] = product[:, place * TILE : (place + 1) * TILE]
        return carry

    lax.fori_loop(0, blocks_dev, gradient_terms, 0, unroll=4)

    def summed(device):
        total = terms[inverse[device, 0]]
        for row_block in range(1, blocks_dev):
            total = total + terms[inverse[device, row_block]]
        return total

    def send_sum(device):
        sums[device] = summed(device).astype(sums.dtype)
        to_dp(sums.at[device], incoming, grad_send, grad_recv, device).start()

    others(send_sum)
    own = summed(me)
    own_choice = choice[me, me]
    for block in range(blocks_owned):
        gradient[block] = (own_choice == block).astype(F32) * own

    lineage[group] = positions[...]
    for offset in range(1, groups):
        position_copy(offset, True).wait_recv()
    for block in range(blocks_owned):
        span = slice(block * TILE, (block + 1) * TILE)
        rows = lineage[:, :, span].reshape(groups * particles, TILE)
        high = rows.astype(BF16)
        low = (rows - high.astype(F32)).astype(BF16)
        resampled[block] = jnp.dot(hot, high, preferred_element_type=F32) + jnp.dot(
            hot, low, preferred_element_type=F32
        )

    for start in range(1, width, ARRIVALS):
        devices = [
            lax.rem(me + offset, width) for offset in range(start, min(start + ARRIVALS, width))
        ]
        for device in devices:
            from_dp(sums.at[device], incoming, grad_send, grad_recv, device).wait_recv()
        arrived = [(choice[device, me], incoming[device].astype(F32)) for device in devices]
        for block in range(blocks_owned):
            total = gradient[block]
            for chosen, value in arrived:
                total = total + (chosen == block).astype(F32) * value
            gradient[block] = total
    for block in range(blocks_owned):
        kept = resampled[block]
        moved = kept + STEP_SIZE * (gradient[block] - PRIOR_PRECISION * kept)
        advanced[:, block * TILE : (block + 1) * TILE] = moved
        narrow[block] = moved.astype(BF16)

    def send_new(device):
        outgoing_new[device] = narrow[choice[device, me]]
        to_dp(outgoing_new.at[device], fetched_new, new_send, new_recv, device).start()

    others(send_new)
    store = pltpu.make_async_copy(advanced, advanced_out, store_sem)
    store.start()
    fetched_new[me] = narrow[choice[me, me]]
    others(
        lambda device: from_dp(
            outgoing_new.at[device], fetched_new, new_send, new_recv, device
        ).wait_recv()
    )

    def likelihood(row_block, carry):
        total, counted = carry
        _, logits, target, section = logits_of(fetched_new, row_block)
        chosen = section == CURRENT + 1
        softplus = jnp.maximum(logits, 0.0) + jnp.log(1.0 + jnp.exp(-jnp.abs(logits)))
        return (
            total + jnp.where(chosen, target * logits - softplus, 0.0),
            counted + chosen.astype(F32),
        )

    total, counted = lax.fori_loop(
        0,
        blocks_dev,
        likelihood,
        (jnp.zeros((particles, TILE), F32), jnp.zeros((1, TILE), F32)),
        unroll=4,
    )
    both = jnp.concatenate([total, jnp.broadcast_to(counted, (particles, TILE))], axis=0)
    row = jnp.sum(both.T, axis=0, keepdims=True)
    row = jnp.broadcast_to(row, totals_own.shape)
    totals_own[...] = row
    totals_all[me] = row
    others(lambda device: to_dp(totals_own, totals_all, tot_send, tot_recv, device).start())
    others(lambda device: from_dp(totals_own, totals_all, tot_send, tot_recv, device).wait_recv())
    final = jnp.sum(totals_all[...], axis=0)
    mean_out[...] = final[:1, :particles] / jnp.maximum(final[:1, particles:], 1.0)

    def wait_sends(device):
        to_dp(outgoing.at[device], fetched, out_send, out_recv, device).wait_send()
        to_dp(sums.at[device], incoming, grad_send, grad_recv, device).wait_send()
        to_dp(outgoing_new.at[device], fetched_new, new_send, new_recv, device).wait_send()
        to_dp(totals_own, totals_all, tot_send, tot_recv, device).wait_send()

    others(wait_sends)
    store.wait()

    def wait_dom(device, carry):
        for offset in range(1, groups):
            dom_copy(device, offset, False).wait_send()
        return carry

    lax.fori_loop(0, width, wait_dom, 0)
    for offset in range(1, groups):
        position_copy(offset, False).wait_send()


def shards(positions, ancestors, block_choice, tile_slot, design, labels, row_section):
    width, groups = lax.axis_size("dp"), lax.axis_size("dom")
    particles, features = positions.shape
    blocks_owned = features // TILE
    blocks_dev, per_block = tile_slot.shape
    tiles = blocks_dev * per_block

    hbm = pl.BlockSpec(memory_space=pl.ANY)
    vmem = pl.BlockSpec(memory_space=pltpu.VMEM)
    block = (particles, TILE)
    dma = pltpu.SemaphoreType.DMA
    advanced, mean = pl.pallas_call(
        functools.partial(round_kernel, groups, width),
        out_shape=(
            jax.ShapeDtypeStruct((particles, features), F32),
            jax.ShapeDtypeStruct((1, particles), F32),
        ),
        in_specs=[hbm] * 7,
        out_specs=(hbm, vmem),
        scratch_shapes=[
            pltpu.SMEM((width, width), jnp.int32),
            pltpu.SMEM((per_block, blocks_dev), jnp.int32),
            pltpu.VMEM((per_block, blocks_dev), jnp.int32),
            pltpu.VMEM((width, blocks_dev), jnp.int32),
            pltpu.SMEM((width, blocks_dev), jnp.int32),
            pltpu.VMEM((particles, features), F32),
            pltpu.VMEM((1, particles), jnp.int32),
            pltpu.VMEM((blocks_dev, TILE), jnp.int32),
            pltpu.VMEM((blocks_dev, TILE), jnp.int32),
            pltpu.VMEM((particles, features), F32),
            pltpu.VMEM((blocks_owned, *block), F32),
            pltpu.VMEM(design.shape, BF16),
            pltpu.VMEM((blocks_owned, *block), BF16),
            pltpu.VMEM((width, *block), BF16),
            pltpu.VMEM((groups, width, *block), BF16),
            pltpu.VMEM((groups, particles, features), F32),
            pltpu.VMEM((blocks_owned, *block), F32),
            pltpu.VMEM((width, *block), BF16),
            pltpu.VMEM((width, *block), BF16),
            pltpu.VMEM((tiles + 1, *block), F32),
            pltpu.VMEM((width, *block), TERM),
            pltpu.VMEM((width, *block), TERM),
            pltpu.VMEM((width, *block), BF16),
            pltpu.VMEM((width, *block), BF16),
            pltpu.VMEM((8, 2 * particles), F32),
            pltpu.VMEM((width, 8, 2 * particles), F32),
            dma((8,)),
            dma,
            dma,
            dma((max(groups - 1, 1), width)),
            dma((max(groups - 1, 1), width)),
            dma((max(groups - 1, 1),)),
            dma((max(groups - 1, 1),)),
            dma((width,)),
            dma((width,)),
            dma((width,)),
            dma((width,)),
            dma((width,)),
            dma((width,)),
            dma((width,)),
            dma((width,)),
        ],
        compiler_params=pltpu.CompilerParams(
            collective_id=0, has_side_effects=True, vmem_limit_bytes=60 << 20
        ),
        name="smc_round",
    )(
        block_choice,
        tile_slot.T,
        positions,
        ancestors.reshape(1, particles),
        design,
        labels.reshape(blocks_dev, TILE),
        row_section.reshape(blocks_dev, TILE),
    )
    return advanced, mean.reshape(particles)


def solution(mesh):
    return jax.shard_map(
        shards,
        mesh=mesh,
        in_specs=(P("dom", "dp"), P("dom"), P(), P("dp", None), P("dp", None), P("dp"), P("dp")),
        out_specs=(P("dom", "dp"), P("dom")),
        check_vma=False,
    )
```

```python
import functools

import jax
import jax.numpy as jnp
from jax import lax
from jax.experimental import pallas as pl
from jax.experimental.pallas import tpu as pltpu
from jax.sharding import PartitionSpec as P

TILE = 128
CURRENT = 2
STEP_SIZE = 1.0
PRIOR_PRECISION = 0.05
ARRIVALS = 4
LEVELS = 32767.0
TINY = 1e-30
MESH = pl.DeviceIdType.MESH
F32, BF16 = jnp.float32, jnp.bfloat16


def round_kernel(
    groups,
    width,
    choice_in,
    slots_in,
    positions_in,
    ancestors_in,
    design_in,
    labels_in,
    sections_in,
    advanced_out,
    mean_out,
    choice,
    slots,
    slots_wide,
    inverse_wide,
    inverse,
    positions,
    ancestors,
    labels,
    sections,
    advanced,
    gradient,
    design,
    narrow,
    picked,
    picked_all,
    lineage,
    resampled,
    outgoing,
    fetched,
    terms,
    sums,
    incoming,
    peaks,
    peaks_in,
    outgoing_new,
    fetched_new,
    totals_own,
    totals_all,
    load_sem,
    inverse_sem,
    store_sem,
    dom_send,
    dom_recv,
    pos_send,
    pos_recv,
    out_send,
    out_recv,
    grad_send,
    grad_recv,
    peak_send,
    peak_recv,
    new_send,
    new_recv,
    tot_send,
    tot_recv,
):
    me, group = lax.axis_index("dp"), lax.axis_index("dom")
    particles = positions.shape[0]
    blocks_owned = positions.shape[1] // TILE
    per_block, blocks_dev = slots.shape
    loads = [
        pltpu.make_async_copy(source, target, load_sem.at[number])
        for number, (source, target) in enumerate(
            (
                (positions_in, positions),
                (choice_in, choice),
                (slots_in, slots_wide),
                (ancestors_in, ancestors),
                (slots_in, slots),
                (labels_in, labels),
                (sections_in, sections),
                (design_in, design),
            )
        )
    ]
    for load in loads:
        load.start()

    def to_dp(source, target, sends, receives, device):
        return pltpu.make_async_remote_copy(
            src_ref=source,
            dst_ref=target.at[me],
            send_sem=sends.at[device],
            recv_sem=receives.at[me],
            device_id=(group, device),
            device_id_type=MESH,
        )

    def from_dp(source, target, sends, receives, device):
        return pltpu.make_async_remote_copy(
            src_ref=source,
            dst_ref=target.at[device],
            send_sem=sends.at[device],
            recv_sem=receives.at[device],
            device_id=(group, device),
            device_id_type=MESH,
        )

    def others(body):
        def step(offset, carry):
            body(lax.rem(me + offset, width))
            return carry

        lax.fori_loop(1, width, step, 0)

    barrier = pltpu.get_barrier_semaphore()

    def greet(device):
        pl.semaphore_signal(barrier, inc=1, device_id=(group, device), device_id_type=MESH)

    others(greet)
    for offset in range(1, groups):
        pl.semaphore_signal(
            barrier, inc=1, device_id=(lax.rem(group + offset, groups), me), device_id_type=MESH
        )
    for load in loads[:4]:
        load.wait()
    for block in range(blocks_owned):
        narrow[block] = positions[:, block * TILE : (block + 1) * TILE].astype(BF16)

    def pick(device, carry):
        value = narrow[choice[device, me]]
        picked[device] = value
        picked_all[group, device] = value
        return carry

    lax.fori_loop(0, width, pick, 0)
    origin = lax.broadcasted_iota(jnp.int32, (groups * particles, particles), 0)
    hot = (origin == ancestors[...]).astype(F32).T.astype(BF16)
    tiles_dev = blocks_dev * per_block
    owner = lax.broadcasted_iota(jnp.int32, (width, blocks_dev), 0)
    first = lax.broadcasted_iota(jnp.int32, (width, blocks_dev), 1) * per_block
    found = jnp.full((width, blocks_dev), tiles_dev, jnp.int32)
    for place in range(per_block):
        found = jnp.where(slots_wide[place : place + 1, :] == owner, first + place, found)
    inverse_wide[...] = found
    inverse_copy = pltpu.make_async_copy(inverse_wide, inverse, inverse_sem)
    inverse_copy.start()
    pl.semaphore_wait(barrier, width + groups - 2)

    def dom_copy(device, offset, incoming_side):
        sign = groups - offset if incoming_side else offset
        peer = lax.rem(group + sign, groups)
        return pltpu.make_async_remote_copy(
            src_ref=picked.at[device],
            dst_ref=picked_all.at[peer if incoming_side else group, device],
            send_sem=dom_send.at[offset - 1, device],
            recv_sem=dom_recv.at[offset - 1, device],
            device_id=(peer, me),
            device_id_type=MESH,
        )

    def position_copy(offset, incoming_side):
        sign = groups - offset if incoming_side else offset
        peer = lax.rem(group + sign, groups)
        return pltpu.make_async_remote_copy(
            src_ref=positions,
            dst_ref=lineage.at[peer if incoming_side else group],
            send_sem=pos_send.at[offset - 1],
            recv_sem=pos_recv.at[offset - 1],
            device_id=(peer, me),
            device_id_type=MESH,
        )

    def send_picked(device):
        for offset in range(1, groups):
            dom_copy(device, offset, False).start()

    others(send_picked)
    send_picked(me)
    for offset in range(1, groups):
        position_copy(offset, False).start()

    def resample(device):
        for offset in range(1, groups):
            dom_copy(device, offset, True).wait_recv()
        rows = picked_all[:, device].reshape(groups * particles, TILE)
        return jnp.dot(hot, rows, preferred_element_type=F32).astype(BF16)

    def send_resampled(device):
        outgoing[device] = resample(device)
        to_dp(outgoing.at[device], fetched, out_send, out_recv, device).start()

    others(send_resampled)
    fetched[me] = resample(me)
    terms[tiles_dev] = jnp.zeros((particles, TILE), F32)
    for load in loads[4:]:
        load.wait()
    inverse_copy.wait()
    others(lambda device: from_dp(outgoing.at[device], fetched, out_send, out_recv, device).wait_recv())

    def logits_of(source, row_block):
        weights = jnp.concatenate(
            [source[slots[place, row_block]] for place in range(per_block)], axis=1
        )
        tiles = design[pl.ds(pl.multiple_of(row_block * TILE, TILE), TILE), :]
        logits = lax.dot_general(
            weights, tiles, (((1,), (1,)), ((), ())), preferred_element_type=F32
        )
        target = labels[pl.ds(row_block, 1), :].astype(F32)
        section = sections[pl.ds(row_block, 1), :]
        return tiles, logits, target, section

    def gradient_terms(row_block, carry):
        tiles, logits, target, section = logits_of(fetched, row_block)
        residual = jnp.where(section <= CURRENT, target - jax.nn.sigmoid(logits), 0.0).astype(BF16)
        product = jnp.dot(residual, tiles, preferred_element_type=F32)
        for place in range(per_block):
            terms[row_block * per_block + place] = product[:, place * TILE : (place + 1) * TILE]
        return carry

    lax.fori_loop(0, blocks_dev, gradient_terms, 0, unroll=4)

    def summed(device):
        total = terms[inverse[device, 0]]
        for row_block in range(1, blocks_dev):
            total = total + terms[inverse[device, row_block]]
        return total

    def send_sum(device):
        total = summed(device)
        peak = jnp.max(jnp.abs(total), axis=0, keepdims=True)
        peaks[device] = peak
        to_dp(peaks.at[device], peaks_in, peak_send, peak_recv, device).start()
        coded = jnp.round(total * (LEVELS / jnp.maximum(peak, TINY)))
        sums[device] = coded.astype(jnp.int32).astype(jnp.int16)
        to_dp(sums.at[device], incoming, grad_send, grad_recv, device).start()

    others(send_sum)
    own = summed(me)
    own_choice = choice[me, me]
    for block in range(blocks_owned):
        gradient[block] = (own_choice == block).astype(F32) * own

    lineage[group] = positions[...]
    for offset in range(1, groups):
        position_copy(offset, True).wait_recv()
    for block in range(blocks_owned):
        span = slice(block * TILE, (block + 1) * TILE)
        rows = lineage[:, :, span].reshape(groups * particles, TILE)
        high = rows.astype(BF16)
        low = (rows - high.astype(F32)).astype(BF16)
        resampled[block] = jnp.dot(hot, high, preferred_element_type=F32) + jnp.dot(
            hot, low, preferred_element_type=F32
        )

    for start in range(1, width, ARRIVALS):
        devices = [
            lax.rem(me + offset, width) for offset in range(start, min(start + ARRIVALS, width))
        ]
        for device in devices:
            from_dp(peaks.at[device], peaks_in, peak_send, peak_recv, device).wait_recv()
            from_dp(sums.at[device], incoming, grad_send, grad_recv, device).wait_recv()
        arrived = [
            (
                choice[device, me],
                incoming[device].astype(jnp.int32).astype(F32)
                * (jnp.maximum(peaks_in[device], TINY) * (1.0 / LEVELS)),
            )
            for device in devices
        ]
        for block in range(blocks_owned):
            total = gradient[block]
            for chosen, value in arrived:
                total = total + (chosen == block).astype(F32) * value
            gradient[block] = total
    for block in range(blocks_owned):
        kept = resampled[block]
        moved = kept + STEP_SIZE * (gradient[block] - PRIOR_PRECISION * kept)
        advanced[:, block * TILE : (block + 1) * TILE] = moved
        narrow[block] = moved.astype(BF16)

    def send_new(device):
        outgoing_new[device] = narrow[choice[device, me]]
        to_dp(outgoing_new.at[device], fetched_new, new_send, new_recv, device).start()

    others(send_new)
    store = pltpu.make_async_copy(advanced, advanced_out, store_sem)
    store.start()
    fetched_new[me] = narrow[choice[me, me]]
    others(
        lambda device: from_dp(
            outgoing_new.at[device], fetched_new, new_send, new_recv, device
        ).wait_recv()
    )

    def likelihood(row_block, carry):
        total, counted = carry
        _, logits, target, section = logits_of(fetched_new, row_block)
        chosen = section == CURRENT + 1
        softplus = jnp.maximum(logits, 0.0) + jnp.log(1.0 + jnp.exp(-jnp.abs(logits)))
        return (
            total + jnp.where(chosen, target * logits - softplus, 0.0),
            counted + chosen.astype(F32),
        )

    total, counted = lax.fori_loop(
        0,
        blocks_dev,
        likelihood,
        (jnp.zeros((particles, TILE), F32), jnp.zeros((1, TILE), F32)),
        unroll=4,
    )
    both = jnp.concatenate([total, jnp.broadcast_to(counted, (particles, TILE))], axis=0)
    row = jnp.sum(both.T, axis=0, keepdims=True)
    row = jnp.broadcast_to(row, totals_own.shape)
    totals_own[...] = row
    totals_all[me] = row
    others(lambda device: to_dp(totals_own, totals_all, tot_send, tot_recv, device).start())
    others(lambda device: from_dp(totals_own, totals_all, tot_send, tot_recv, device).wait_recv())
    final = jnp.sum(totals_all[...], axis=0)
    mean_out[...] = final[:1, :particles] / jnp.maximum(final[:1, particles:], 1.0)

    def wait_sends(device):
        to_dp(outgoing.at[device], fetched, out_send, out_recv, device).wait_send()
        to_dp(sums.at[device], incoming, grad_send, grad_recv, device).wait_send()
        to_dp(peaks.at[device], peaks_in, peak_send, peak_recv, device).wait_send()
        to_dp(outgoing_new.at[device], fetched_new, new_send, new_recv, device).wait_send()
        to_dp(totals_own, totals_all, tot_send, tot_recv, device).wait_send()

    others(wait_sends)
    store.wait()

    def wait_dom(device, carry):
        for offset in range(1, groups):
            dom_copy(device, offset, False).wait_send()
        return carry

    lax.fori_loop(0, width, wait_dom, 0)
    for offset in range(1, groups):
        position_copy(offset, False).wait_send()


def shards(positions, ancestors, block_choice, tile_slot, design, labels, row_section):
    width, groups = lax.axis_size("dp"), lax.axis_size("dom")
    particles, features = positions.shape
    blocks_owned = features // TILE
    blocks_dev, per_block = tile_slot.shape
    tiles = blocks_dev * per_block

    hbm = pl.BlockSpec(memory_space=pl.ANY)
    vmem = pl.BlockSpec(memory_space=pltpu.VMEM)
    block = (particles, TILE)
    dma = pltpu.SemaphoreType.DMA
    advanced, mean = pl.pallas_call(
        functools.partial(round_kernel, groups, width),
        out_shape=(
            jax.ShapeDtypeStruct((particles, features), F32),
            jax.ShapeDtypeStruct((1, particles), F32),
        ),
        in_specs=[hbm] * 7,
        out_specs=(hbm, vmem),
        scratch_shapes=[
            pltpu.SMEM((width, width), jnp.int32),
            pltpu.SMEM((per_block, blocks_dev), jnp.int32),
            pltpu.VMEM((per_block, blocks_dev), jnp.int32),
            pltpu.VMEM((width, blocks_dev), jnp.int32),
            pltpu.SMEM((width, blocks_dev), jnp.int32),
            pltpu.VMEM((particles, features), F32),
            pltpu.VMEM((1, particles), jnp.int32),
            pltpu.VMEM((blocks_dev, TILE), jnp.int32),
            pltpu.VMEM((blocks_dev, TILE), jnp.int32),
            pltpu.VMEM((particles, features), F32),
            pltpu.VMEM((blocks_owned, *block), F32),
            pltpu.VMEM(design.shape, BF16),
            pltpu.VMEM((blocks_owned, *block), BF16),
            pltpu.VMEM((width, *block), BF16),
            pltpu.VMEM((groups, width, *block), BF16),
            pltpu.VMEM((groups, particles, features), F32),
            pltpu.VMEM((blocks_owned, *block), F32),
            pltpu.VMEM((width, *block), BF16),
            pltpu.VMEM((width, *block), BF16),
            pltpu.VMEM((tiles + 1, *block), F32),
            pltpu.VMEM((width, *block), jnp.int16),
            pltpu.VMEM((width, *block), jnp.int16),
            pltpu.VMEM((width, 1, TILE), F32),
            pltpu.VMEM((width, 1, TILE), F32),
            pltpu.VMEM((width, *block), BF16),
            pltpu.VMEM((width, *block), BF16),
            pltpu.VMEM((8, 2 * particles), F32),
            pltpu.VMEM((width, 8, 2 * particles), F32),
            dma((8,)),
            dma,
            dma,
            dma((max(groups - 1, 1), width)),
            dma((max(groups - 1, 1), width)),
            dma((max(groups - 1, 1),)),
            dma((max(groups - 1, 1),)),
            dma((width,)),
            dma((width,)),
            dma((width,)),
            dma((width,)),
            dma((width,)),
            dma((width,)),
            dma((width,)),
            dma((width,)),
            dma((width,)),
            dma((width,)),
        ],
        compiler_params=pltpu.CompilerParams(
            collective_id=0, has_side_effects=True, vmem_limit_bytes=60 << 20
        ),
        name="smc_round",
    )(
        block_choice,
        tile_slot.T,
        positions,
        ancestors.reshape(1, particles),
        design,
        labels.reshape(blocks_dev, TILE),
        row_section.reshape(blocks_dev, TILE),
    )
    return advanced, mean.reshape(particles)


def solution(mesh):
    return jax.shard_map(
        shards,
        mesh=mesh,
        in_specs=(P("dom", "dp"), P("dom"), P(), P("dp", None), P("dp", None), P("dp"), P("dp")),
        out_specs=(P("dom", "dp"), P("dom")),
        check_vma=False,
    )
```

```python
import functools

import jax
import jax.numpy as jnp
from jax import lax
from jax.experimental import pallas as pl
from jax.experimental.pallas import tpu as pltpu
from jax.sharding import PartitionSpec as P

TILE = 128
CURRENT = 2
STEP_SIZE = 1.0
PRIOR_PRECISION = 0.05
ARRIVALS = 4
LEVELS = 32767.0
TINY = 1e-30
MESH = pl.DeviceIdType.MESH
F32, BF16 = jnp.float32, jnp.bfloat16


def far_first(turn, width):
    odd = turn % 2
    return width // 2 + odd * ((turn + 1) // 2) - (1 - odd) * (turn // 2) if width % 2 == 0 else turn + 1


def round_kernel(
    groups,
    width,
    choice_in,
    slots_in,
    positions_in,
    ancestors_in,
    design_in,
    labels_in,
    sections_in,
    advanced_out,
    mean_out,
    choice,
    slots,
    slots_wide,
    inverse_wide,
    inverse,
    positions,
    ancestors,
    labels,
    sections,
    advanced,
    gradient,
    design,
    narrow,
    picked,
    picked_all,
    lineage,
    resampled,
    outgoing,
    fetched,
    terms,
    sums,
    incoming,
    peaks,
    peaks_in,
    outgoing_new,
    fetched_new,
    totals_own,
    totals_all,
    load_sem,
    inverse_sem,
    store_sem,
    dom_send,
    dom_recv,
    pos_send,
    pos_recv,
    out_send,
    out_recv,
    grad_send,
    grad_recv,
    peak_send,
    peak_recv,
    new_send,
    new_recv,
    tot_send,
    tot_recv,
):
    me, group = lax.axis_index("dp"), lax.axis_index("dom")
    particles = positions.shape[0]
    blocks_owned = positions.shape[1] // TILE
    per_block, blocks_dev = slots.shape
    loads = [
        pltpu.make_async_copy(source, target, load_sem.at[number])
        for number, (source, target) in enumerate(
            (
                (positions_in, positions),
                (choice_in, choice),
                (slots_in, slots_wide),
                (ancestors_in, ancestors),
                (slots_in, slots),
                (labels_in, labels),
                (sections_in, sections),
                (design_in, design),
            )
        )
    ]
    for load in loads:
        load.start()

    def to_dp(source, target, sends, receives, device):
        return pltpu.make_async_remote_copy(
            src_ref=source,
            dst_ref=target.at[me],
            send_sem=sends.at[device],
            recv_sem=receives.at[me],
            device_id=(group, device),
            device_id_type=MESH,
        )

    def from_dp(source, target, sends, receives, device):
        return pltpu.make_async_remote_copy(
            src_ref=source,
            dst_ref=target.at[device],
            send_sem=sends.at[device],
            recv_sem=receives.at[device],
            device_id=(group, device),
            device_id_type=MESH,
        )

    def others(body):
        def step(turn, carry):
            body(lax.rem(me + far_first(turn, width), width))
            return carry

        lax.fori_loop(0, width - 1, step, 0)

    barrier = pltpu.get_barrier_semaphore()

    def greet(device):
        pl.semaphore_signal(barrier, inc=1, device_id=(group, device), device_id_type=MESH)

    others(greet)
    for offset in range(1, groups):
        pl.semaphore_signal(
            barrier, inc=1, device_id=(lax.rem(group + offset, groups), me), device_id_type=MESH
        )
    for load in loads[:4]:
        load.wait()
    for block in range(blocks_owned):
        narrow[block] = positions[:, block * TILE : (block + 1) * TILE].astype(BF16)

    def pick(device, carry):
        value = narrow[choice[device, me]]
        picked[device] = value
        picked_all[group, device] = value
        return carry

    lax.fori_loop(0, width, pick, 0)
    origin = lax.broadcasted_iota(jnp.int32, (groups * particles, particles), 0)
    hot = (origin == ancestors[...]).astype(F32).T.astype(BF16)
    tiles_dev = blocks_dev * per_block
    owner = lax.broadcasted_iota(jnp.int32, (width, blocks_dev), 0)
    first = lax.broadcasted_iota(jnp.int32, (width, blocks_dev), 1) * per_block
    found = jnp.full((width, blocks_dev), tiles_dev, jnp.int32)
    for place in range(per_block):
        found = jnp.where(slots_wide[place : place + 1, :] == owner, first + place, found)
    inverse_wide[...] = found
    inverse_copy = pltpu.make_async_copy(inverse_wide, inverse, inverse_sem)
    inverse_copy.start()
    pl.semaphore_wait(barrier, width + groups - 2)

    def dom_copy(device, offset, incoming_side):
        sign = groups - offset if incoming_side else offset
        peer = lax.rem(group + sign, groups)
        return pltpu.make_async_remote_copy(
            src_ref=picked.at[device],
            dst_ref=picked_all.at[peer if incoming_side else group, device],
            send_sem=dom_send.at[offset - 1, device],
            recv_sem=dom_recv.at[offset - 1, device],
            device_id=(peer, me),
            device_id_type=MESH,
        )

    def position_copy(offset, incoming_side):
        sign = groups - offset if incoming_side else offset
        peer = lax.rem(group + sign, groups)
        return pltpu.make_async_remote_copy(
            src_ref=positions,
            dst_ref=lineage.at[peer if incoming_side else group],
            send_sem=pos_send.at[offset - 1],
            recv_sem=pos_recv.at[offset - 1],
            device_id=(peer, me),
            device_id_type=MESH,
        )

    def send_picked(device):
        for offset in range(1, groups):
            dom_copy(device, offset, False).start()

    others(send_picked)
    send_picked(me)
    for offset in range(1, groups):
        position_copy(offset, False).start()

    def resample(device):
        for offset in range(1, groups):
            dom_copy(device, offset, True).wait_recv()
        rows = picked_all[:, device].reshape(groups * particles, TILE)
        return jnp.dot(hot, rows, preferred_element_type=F32).astype(BF16)

    def send_resampled(device):
        outgoing[device] = resample(device)
        to_dp(outgoing.at[device], fetched, out_send, out_recv, device).start()

    others(send_resampled)
    fetched[me] = resample(me)
    terms[tiles_dev] = jnp.zeros((particles, TILE), F32)
    for load in loads[4:]:
        load.wait()
    inverse_copy.wait()
    others(lambda device: from_dp(outgoing.at[device], fetched, out_send, out_recv, device).wait_recv())

    def logits_of(source, row_block):
        weights = jnp.concatenate(
            [source[slots[place, row_block]] for place in range(per_block)], axis=1
        )
        tiles = design[pl.ds(pl.multiple_of(row_block * TILE, TILE), TILE), :]
        logits = lax.dot_general(
            weights, tiles, (((1,), (1,)), ((), ())), preferred_element_type=F32
        )
        target = labels[pl.ds(row_block, 1), :].astype(F32)
        section = sections[pl.ds(row_block, 1), :]
        return tiles, logits, target, section

    def gradient_terms(row_block, carry):
        tiles, logits, target, section = logits_of(fetched, row_block)
        residual = jnp.where(section <= CURRENT, target - jax.nn.sigmoid(logits), 0.0).astype(BF16)
        product = jnp.dot(residual, tiles, preferred_element_type=F32)
        for place in range(per_block):
            terms[row_block * per_block + place] = product[:, place * TILE : (place + 1) * TILE]
        return carry

    lax.fori_loop(0, blocks_dev, gradient_terms, 0, unroll=4)

    def summed(device):
        total = terms[inverse[device, 0]]
        for row_block in range(1, blocks_dev):
            total = total + terms[inverse[device, row_block]]
        return total

    def send_sum(device):
        total = summed(device)
        peak = jnp.max(jnp.abs(total), axis=0, keepdims=True)
        peaks[device] = peak
        to_dp(peaks.at[device], peaks_in, peak_send, peak_recv, device).start()
        coded = jnp.round(total * (LEVELS / jnp.maximum(peak, TINY)))
        sums[device] = coded.astype(jnp.int32).astype(jnp.int16)
        to_dp(sums.at[device], incoming, grad_send, grad_recv, device).start()

    others(send_sum)
    own = summed(me)
    own_choice = choice[me, me]
    for block in range(blocks_owned):
        gradient[block] = (own_choice == block).astype(F32) * own

    lineage[group] = positions[...]
    for offset in range(1, groups):
        position_copy(offset, True).wait_recv()
    for block in range(blocks_owned):
        span = slice(block * TILE, (block + 1) * TILE)
        rows = lineage[:, :, span].reshape(groups * particles, TILE)
        high = rows.astype(BF16)
        low = (rows - high.astype(F32)).astype(BF16)
        resampled[block] = jnp.dot(hot, high, preferred_element_type=F32) + jnp.dot(
            hot, low, preferred_element_type=F32
        )

    for start in range(0, width - 1, ARRIVALS):
        devices = [
            lax.rem(me + far_first(turn, width), width)
            for turn in range(start, min(start + ARRIVALS, width - 1))
        ]
        for device in devices:
            from_dp(peaks.at[device], peaks_in, peak_send, peak_recv, device).wait_recv()
            from_dp(sums.at[device], incoming, grad_send, grad_recv, device).wait_recv()
        arrived = [
            (
                choice[device, me],
                incoming[device].astype(jnp.int32).astype(F32)
                * (jnp.maximum(peaks_in[device], TINY) * (1.0 / LEVELS)),
            )
            for device in devices
        ]
        for block in range(blocks_owned):
            total = gradient[block]
            for chosen, value in arrived:
                total = total + (chosen == block).astype(F32) * value
            gradient[block] = total
    for block in range(blocks_owned):
        kept = resampled[block]
        moved = kept + STEP_SIZE * (gradient[block] - PRIOR_PRECISION * kept)
        advanced[:, block * TILE : (block + 1) * TILE] = moved
        narrow[block] = moved.astype(BF16)

    def send_new(device):
        outgoing_new[device] = narrow[choice[device, me]]
        to_dp(outgoing_new.at[device], fetched_new, new_send, new_recv, device).start()

    others(send_new)
    store = pltpu.make_async_copy(advanced, advanced_out, store_sem)
    store.start()
    fetched_new[me] = narrow[choice[me, me]]
    others(
        lambda device: from_dp(
            outgoing_new.at[device], fetched_new, new_send, new_recv, device
        ).wait_recv()
    )

    def likelihood(row_block, carry):
        total, counted = carry
        _, logits, target, section = logits_of(fetched_new, row_block)
        chosen = section == CURRENT + 1
        softplus = jnp.maximum(logits, 0.0) + jnp.log(1.0 + jnp.exp(-jnp.abs(logits)))
        return (
            total + jnp.where(chosen, target * logits - softplus, 0.0),
            counted + chosen.astype(F32),
        )

    total, counted = lax.fori_loop(
        0,
        blocks_dev,
        likelihood,
        (jnp.zeros((particles, TILE), F32), jnp.zeros((1, TILE), F32)),
        unroll=4,
    )
    both = jnp.concatenate([total, jnp.broadcast_to(counted, (particles, TILE))], axis=0)
    row = jnp.sum(both.T, axis=0, keepdims=True)
    row = jnp.broadcast_to(row, totals_own.shape)
    totals_own[...] = row
    totals_all[me] = row
    others(lambda device: to_dp(totals_own, totals_all, tot_send, tot_recv, device).start())
    others(lambda device: from_dp(totals_own, totals_all, tot_send, tot_recv, device).wait_recv())
    final = jnp.sum(totals_all[...], axis=0)
    mean_out[...] = final[:1, :particles] / jnp.maximum(final[:1, particles:], 1.0)

    def wait_sends(device):
        to_dp(outgoing.at[device], fetched, out_send, out_recv, device).wait_send()
        to_dp(sums.at[device], incoming, grad_send, grad_recv, device).wait_send()
        to_dp(peaks.at[device], peaks_in, peak_send, peak_recv, device).wait_send()
        to_dp(outgoing_new.at[device], fetched_new, new_send, new_recv, device).wait_send()
        to_dp(totals_own, totals_all, tot_send, tot_recv, device).wait_send()

    others(wait_sends)
    store.wait()

    def wait_dom(device, carry):
        for offset in range(1, groups):
            dom_copy(device, offset, False).wait_send()
        return carry

    lax.fori_loop(0, width, wait_dom, 0)
    for offset in range(1, groups):
        position_copy(offset, False).wait_send()


def shards(positions, ancestors, block_choice, tile_slot, design, labels, row_section):
    width, groups = lax.axis_size("dp"), lax.axis_size("dom")
    particles, features = positions.shape
    blocks_owned = features // TILE
    blocks_dev, per_block = tile_slot.shape
    tiles = blocks_dev * per_block

    hbm = pl.BlockSpec(memory_space=pl.ANY)
    vmem = pl.BlockSpec(memory_space=pltpu.VMEM)
    block = (particles, TILE)
    dma = pltpu.SemaphoreType.DMA
    advanced, mean = pl.pallas_call(
        functools.partial(round_kernel, groups, width),
        out_shape=(
            jax.ShapeDtypeStruct((particles, features), F32),
            jax.ShapeDtypeStruct((1, particles), F32),
        ),
        in_specs=[hbm] * 7,
        out_specs=(hbm, vmem),
        scratch_shapes=[
            pltpu.SMEM((width, width), jnp.int32),
            pltpu.SMEM((per_block, blocks_dev), jnp.int32),
            pltpu.VMEM((per_block, blocks_dev), jnp.int32),
            pltpu.VMEM((width, blocks_dev), jnp.int32),
            pltpu.SMEM((width, blocks_dev), jnp.int32),
            pltpu.VMEM((particles, features), F32),
            pltpu.VMEM((1, particles), jnp.int32),
            pltpu.VMEM((blocks_dev, TILE), jnp.int32),
            pltpu.VMEM((blocks_dev, TILE), jnp.int32),
            pltpu.VMEM((particles, features), F32),
            pltpu.VMEM((blocks_owned, *block), F32),
            pltpu.VMEM(design.shape, BF16),
            pltpu.VMEM((blocks_owned, *block), BF16),
            pltpu.VMEM((width, *block), BF16),
            pltpu.VMEM((groups, width, *block), BF16),
            pltpu.VMEM((groups, particles, features), F32),
            pltpu.VMEM((blocks_owned, *block), F32),
            pltpu.VMEM((width, *block), BF16),
            pltpu.VMEM((width, *block), BF16),
            pltpu.VMEM((tiles + 1, *block), F32),
            pltpu.VMEM((width, *block), jnp.int16),
            pltpu.VMEM((width, *block), jnp.int16),
            pltpu.VMEM((width, 1, TILE), F32),
            pltpu.VMEM((width, 1, TILE), F32),
            pltpu.VMEM((width, *block), BF16),
            pltpu.VMEM((width, *block), BF16),
            pltpu.VMEM((8, 2 * particles), F32),
            pltpu.VMEM((width, 8, 2 * particles), F32),
            dma((8,)),
            dma,
            dma,
            dma((max(groups - 1, 1), width)),
            dma((max(groups - 1, 1), width)),
            dma((max(groups - 1, 1),)),
            dma((max(groups - 1, 1),)),
            dma((width,)),
            dma((width,)),
            dma((width,)),
            dma((width,)),
            dma((width,)),
            dma((width,)),
            dma((width,)),
            dma((width,)),
            dma((width,)),
            dma((width,)),
        ],
        compiler_params=pltpu.CompilerParams(
            collective_id=0, has_side_effects=True, vmem_limit_bytes=60 << 20
        ),
        name="smc_round",
    )(
        block_choice,
        tile_slot.T,
        positions,
        ancestors.reshape(1, particles),
        design,
        labels.reshape(blocks_dev, TILE),
        row_section.reshape(blocks_dev, TILE),
    )
    return advanced, mean.reshape(particles)


def solution(mesh):
    return jax.shard_map(
        shards,
        mesh=mesh,
        in_specs=(P("dom", "dp"), P("dom"), P(), P("dp", None), P("dp", None), P("dp"), P("dp")),
        out_specs=(P("dom", "dp"), P("dom")),
        check_vma=False,
    )
```

```python
import functools

import jax
import jax.numpy as jnp
from jax import lax
from jax.experimental import pallas as pl
from jax.experimental.pallas import tpu as pltpu
from jax.sharding import PartitionSpec as P

TILE = 128
CURRENT = 2
STEP_SIZE = 1.0
PRIOR_PRECISION = 0.05
ARRIVALS = 4
LEVELS = 32767.0
TINY = 1e-30
MESH = pl.DeviceIdType.MESH
F32, BF16 = jnp.float32, jnp.bfloat16


def round_kernel(
    groups,
    width,
    choice_in,
    slots_in,
    positions_in,
    ancestors_in,
    design_in,
    labels_in,
    sections_in,
    advanced_out,
    mean_out,
    choice,
    slots,
    slots_wide,
    inverse_wide,
    inverse,
    positions,
    ancestors,
    labels,
    sections,
    advanced,
    gradient,
    design,
    narrow,
    picked,
    picked_all,
    lineage,
    resampled,
    outgoing,
    fetched,
    residual,
    terms,
    sums,
    incoming,
    peaks,
    peaks_in,
    outgoing_new,
    fetched_new,
    totals_own,
    totals_all,
    load_sem,
    inverse_sem,
    store_sem,
    dom_send,
    dom_recv,
    pos_send,
    pos_recv,
    out_send,
    out_recv,
    grad_send,
    grad_recv,
    peak_send,
    peak_recv,
    new_send,
    new_recv,
    tot_send,
    tot_recv,
):
    me, group = lax.axis_index("dp"), lax.axis_index("dom")
    particles = positions.shape[0]
    blocks_owned = positions.shape[1] // TILE
    per_block, blocks_dev = slots.shape
    loads = [
        pltpu.make_async_copy(source, target, load_sem.at[number])
        for number, (source, target) in enumerate(
            (
                (positions_in, positions),
                (choice_in, choice),
                (slots_in, slots_wide),
                (ancestors_in, ancestors),
                (slots_in, slots),
                (labels_in, labels),
                (sections_in, sections),
                (design_in, design),
            )
        )
    ]
    for load in loads:
        load.start()

    def to_dp(source, target, sends, receives, device):
        return pltpu.make_async_remote_copy(
            src_ref=source,
            dst_ref=target.at[me],
            send_sem=sends.at[device],
            recv_sem=receives.at[me],
            device_id=(group, device),
            device_id_type=MESH,
        )

    def from_dp(source, target, sends, receives, device):
        return pltpu.make_async_remote_copy(
            src_ref=source,
            dst_ref=target.at[device],
            send_sem=sends.at[device],
            recv_sem=receives.at[device],
            device_id=(group, device),
            device_id_type=MESH,
        )

    def others(body):
        def step(offset, carry):
            body(lax.rem(me + offset, width))
            return carry

        lax.fori_loop(1, width, step, 0)

    barrier = pltpu.get_barrier_semaphore()

    def greet(device):
        pl.semaphore_signal(barrier, inc=1, device_id=(group, device), device_id_type=MESH)

    others(greet)
    for offset in range(1, groups):
        pl.semaphore_signal(
            barrier, inc=1, device_id=(lax.rem(group + offset, groups), me), device_id_type=MESH
        )
    for load in loads[:4]:
        load.wait()
    for block in range(blocks_owned):
        narrow[block] = positions[:, block * TILE : (block + 1) * TILE].astype(BF16)

    def pick(device, carry):
        value = narrow[choice[device, me]]
        picked[device] = value
        picked_all[group, device] = value
        return carry

    lax.fori_loop(0, width, pick, 0)
    origin = lax.broadcasted_iota(jnp.int32, (groups * particles, particles), 0)
    hot = (origin == ancestors[...]).astype(F32).T.astype(BF16)
    tiles_dev = blocks_dev * per_block
    owner = lax.broadcasted_iota(jnp.int32, (width, blocks_dev), 0)
    first = lax.broadcasted_iota(jnp.int32, (width, blocks_dev), 1) * per_block
    found = jnp.full((width, blocks_dev), tiles_dev, jnp.int32)
    for place in range(per_block):
        found = jnp.where(slots_wide[place : place + 1, :] == owner, first + place, found)
    inverse_wide[...] = found
    inverse_copy = pltpu.make_async_copy(inverse_wide, inverse, inverse_sem)
    inverse_copy.start()
    pl.semaphore_wait(barrier, width + groups - 2)

    def dom_copy(device, offset, incoming_side):
        sign = groups - offset if incoming_side else offset
        peer = lax.rem(group + sign, groups)
        return pltpu.make_async_remote_copy(
            src_ref=picked.at[device],
            dst_ref=picked_all.at[peer if incoming_side else group, device],
            send_sem=dom_send.at[offset - 1, device],
            recv_sem=dom_recv.at[offset - 1, device],
            device_id=(peer, me),
            device_id_type=MESH,
        )

    def position_copy(offset, incoming_side):
        sign = groups - offset if incoming_side else offset
        peer = lax.rem(group + sign, groups)
        return pltpu.make_async_remote_copy(
            src_ref=positions,
            dst_ref=lineage.at[peer if incoming_side else group],
            send_sem=pos_send.at[offset - 1],
            recv_sem=pos_recv.at[offset - 1],
            device_id=(peer, me),
            device_id_type=MESH,
        )

    def send_picked(device):
        for offset in range(1, groups):
            dom_copy(device, offset, False).start()

    others(send_picked)
    send_picked(me)

    def resample(device):
        for offset in range(1, groups):
            dom_copy(device, offset, True).wait_recv()
        rows = picked_all[:, device].reshape(groups * particles, TILE)
        return jnp.dot(hot, rows, preferred_element_type=F32).astype(BF16)

    def send_resampled(device):
        outgoing[device] = resample(device)
        to_dp(outgoing.at[device], fetched, out_send, out_recv, device).start()

    others(send_resampled)
    fetched[me] = resample(me)
    for offset in range(1, groups):
        position_copy(offset, False).start()
    terms[tiles_dev] = jnp.zeros((particles, TILE), F32)
    for load in loads[4:]:
        load.wait()
    inverse_copy.wait()
    others(lambda device: from_dp(outgoing.at[device], fetched, out_send, out_recv, device).wait_recv())

    def logits_of(source, row_block):
        weights = jnp.concatenate(
            [source[slots[place, row_block]] for place in range(per_block)], axis=1
        )
        tiles = design[pl.ds(pl.multiple_of(row_block * TILE, TILE), TILE), :]
        logits = lax.dot_general(
            weights, tiles, (((1,), (1,)), ((), ())), preferred_element_type=F32
        )
        target = labels[pl.ds(row_block, 1), :].astype(F32)
        section = sections[pl.ds(row_block, 1), :]
        return logits, target, section

    def residuals(row_block, carry):
        logits, target, section = logits_of(fetched, row_block)
        residual[row_block] = jnp.where(
            section <= CURRENT, target - jax.nn.sigmoid(logits), 0.0
        ).astype(BF16)
        return carry

    lax.fori_loop(0, blocks_dev, residuals, 0, unroll=8)

    def gradient_terms(row_block, carry):
        tiles = design[pl.ds(pl.multiple_of(row_block * TILE, TILE), TILE), :]
        product = jnp.dot(residual[row_block], tiles, preferred_element_type=F32)
        for place in range(per_block):
            terms[row_block * per_block + place] = product[:, place * TILE : (place + 1) * TILE]
        return carry

    lax.fori_loop(0, blocks_dev, gradient_terms, 0, unroll=8)

    def summed(device):
        total = terms[inverse[device, 0]]
        for row_block in range(1, blocks_dev):
            total = total + terms[inverse[device, row_block]]
        return total

    def send_sum(device):
        total = summed(device)
        peak = jnp.max(jnp.abs(total), axis=0, keepdims=True)
        peaks[device] = peak
        to_dp(peaks.at[device], peaks_in, peak_send, peak_recv, device).start()
        coded = jnp.round(total * (LEVELS / jnp.maximum(peak, TINY)))
        sums[device] = coded.astype(jnp.int32).astype(jnp.int16)
        to_dp(sums.at[device], incoming, grad_send, grad_recv, device).start()

    others(send_sum)
    own = summed(me)
    own_choice = choice[me, me]
    for block in range(blocks_owned):
        gradient[block] = (own_choice == block).astype(F32) * own

    lineage[group] = positions[...]
    for offset in range(1, groups):
        position_copy(offset, True).wait_recv()
    for block in range(blocks_owned):
        span = slice(block * TILE, (block + 1) * TILE)
        rows = lineage[:, :, span].reshape(groups * particles, TILE)
        high = rows.astype(BF16)
        low = (rows - high.astype(F32)).astype(BF16)
        resampled[block] = jnp.dot(hot, high, preferred_element_type=F32) + jnp.dot(
            hot, low, preferred_element_type=F32
        )

    for start in range(1, width, ARRIVALS):
        devices = [
            lax.rem(me + offset, width) for offset in range(start, min(start + ARRIVALS, width))
        ]
        for device in devices:
            from_dp(peaks.at[device], peaks_in, peak_send, peak_recv, device).wait_recv()
            from_dp(sums.at[device], incoming, grad_send, grad_recv, device).wait_recv()
        arrived = [
            (
                choice[device, me],
                incoming[device].astype(jnp.int32).astype(F32)
                * (jnp.maximum(peaks_in[device], TINY) * (1.0 / LEVELS)),
            )
            for device in devices
        ]
        for block in range(blocks_owned):
            total = gradient[block]
            for chosen, value in arrived:
                total = total + (chosen == block).astype(F32) * value
            gradient[block] = total
    for block in range(blocks_owned):
        kept = resampled[block]
        moved = kept + STEP_SIZE * (gradient[block] - PRIOR_PRECISION * kept)
        advanced[:, block * TILE : (block + 1) * TILE] = moved
        narrow[block] = moved.astype(BF16)

    def send_new(device):
        outgoing_new[device] = narrow[choice[device, me]]
        to_dp(outgoing_new.at[device], fetched_new, new_send, new_recv, device).start()

    others(send_new)
    store = pltpu.make_async_copy(advanced, advanced_out, store_sem)
    store.start()
    fetched_new[me] = narrow[choice[me, me]]
    others(
        lambda device: from_dp(
            outgoing_new.at[device], fetched_new, new_send, new_recv, device
        ).wait_recv()
    )

    def likelihood(row_block, carry):
        total, counted = carry
        logits, target, section = logits_of(fetched_new, row_block)
        chosen = section == CURRENT + 1
        softplus = jnp.maximum(logits, 0.0) + jnp.log(1.0 + jnp.exp(-jnp.abs(logits)))
        return (
            total + jnp.where(chosen, target * logits - softplus, 0.0),
            counted + chosen.astype(F32),
        )

    total, counted = lax.fori_loop(
        0,
        blocks_dev,
        likelihood,
        (jnp.zeros((particles, TILE), F32), jnp.zeros((1, TILE), F32)),
        unroll=8,
    )
    both = jnp.concatenate([total, jnp.broadcast_to(counted, (particles, TILE))], axis=0)
    row = jnp.sum(both.T, axis=0, keepdims=True)
    row = jnp.broadcast_to(row, totals_own.shape)
    totals_own[...] = row
    totals_all[me] = row
    others(lambda device: to_dp(totals_own, totals_all, tot_send, tot_recv, device).start())
    others(lambda device: from_dp(totals_own, totals_all, tot_send, tot_recv, device).wait_recv())
    final = jnp.sum(totals_all[...], axis=0)
    mean_out[...] = final[:1, :particles] / jnp.maximum(final[:1, particles:], 1.0)

    def wait_sends(device):
        to_dp(outgoing.at[device], fetched, out_send, out_recv, device).wait_send()
        to_dp(sums.at[device], incoming, grad_send, grad_recv, device).wait_send()
        to_dp(peaks.at[device], peaks_in, peak_send, peak_recv, device).wait_send()
        to_dp(outgoing_new.at[device], fetched_new, new_send, new_recv, device).wait_send()
        to_dp(totals_own, totals_all, tot_send, tot_recv, device).wait_send()

    others(wait_sends)
    store.wait()

    def wait_dom(device, carry):
        for offset in range(1, groups):
            dom_copy(device, offset, False).wait_send()
        return carry

    lax.fori_loop(0, width, wait_dom, 0)
    for offset in range(1, groups):
        position_copy(offset, False).wait_send()


def shards(positions, ancestors, block_choice, tile_slot, design, labels, row_section):
    width, groups = lax.axis_size("dp"), lax.axis_size("dom")
    particles, features = positions.shape
    blocks_owned = features // TILE
    blocks_dev, per_block = tile_slot.shape
    tiles = blocks_dev * per_block

    hbm = pl.BlockSpec(memory_space=pl.ANY)
    vmem = pl.BlockSpec(memory_space=pltpu.VMEM)
    block = (particles, TILE)
    dma = pltpu.SemaphoreType.DMA
    advanced, mean = pl.pallas_call(
        functools.partial(round_kernel, groups, width),
        out_shape=(
            jax.ShapeDtypeStruct((particles, features), F32),
            jax.ShapeDtypeStruct((1, particles), F32),
        ),
        in_specs=[hbm] * 7,
        out_specs=(hbm, vmem),
        scratch_shapes=[
            pltpu.SMEM((width, width), jnp.int32),
            pltpu.SMEM((per_block, blocks_dev), jnp.int32),
            pltpu.VMEM((per_block, blocks_dev), jnp.int32),
            pltpu.VMEM((width, blocks_dev), jnp.int32),
            pltpu.SMEM((width, blocks_dev), jnp.int32),
            pltpu.VMEM((particles, features), F32),
            pltpu.VMEM((1, particles), jnp.int32),
            pltpu.VMEM((blocks_dev, TILE), jnp.int32),
            pltpu.VMEM((blocks_dev, TILE), jnp.int32),
            pltpu.VMEM((particles, features), F32),
            pltpu.VMEM((blocks_owned, *block), F32),
            pltpu.VMEM(design.shape, BF16),
            pltpu.VMEM((blocks_owned, *block), BF16),
            pltpu.VMEM((width, *block), BF16),
            pltpu.VMEM((groups, width, *block), BF16),
            pltpu.VMEM((groups, particles, features), F32),
            pltpu.VMEM((blocks_owned, *block), F32),
            pltpu.VMEM((width, *block), BF16),
            pltpu.VMEM((width, *block), BF16),
            pltpu.VMEM((blocks_dev, *block), BF16),
            pltpu.VMEM((tiles + 1, *block), F32),
            pltpu.VMEM((width, *block), jnp.int16),
            pltpu.VMEM((width, *block), jnp.int16),
            pltpu.VMEM((width, 1, TILE), F32),
            pltpu.VMEM((width, 1, TILE), F32),
            pltpu.VMEM((width, *block), BF16),
            pltpu.VMEM((width, *block), BF16),
            pltpu.VMEM((8, 2 * particles), F32),
            pltpu.VMEM((width, 8, 2 * particles), F32),
            dma((8,)),
            dma,
            dma,
            dma((max(groups - 1, 1), width)),
            dma((max(groups - 1, 1), width)),
            dma((max(groups - 1, 1),)),
            dma((max(groups - 1, 1),)),
            dma((width,)),
            dma((width,)),
            dma((width,)),
            dma((width,)),
            dma((width,)),
            dma((width,)),
            dma((width,)),
            dma((width,)),
            dma((width,)),
            dma((width,)),
        ],
        compiler_params=pltpu.CompilerParams(
            collective_id=0, has_side_effects=True, vmem_limit_bytes=60 << 20
        ),
        name="smc_round",
    )(
        block_choice,
        tile_slot.T,
        positions,
        ancestors.reshape(1, particles),
        design,
        labels.reshape(blocks_dev, TILE),
        row_section.reshape(blocks_dev, TILE),
    )
    return advanced, mean.reshape(particles)


def solution(mesh):
    return jax.shard_map(
        shards,
        mesh=mesh,
        in_specs=(P("dom", "dp"), P("dom"), P(), P("dp", None), P("dp", None), P("dp"), P("dp")),
        out_specs=(P("dom", "dp"), P("dom")),
        check_vma=False,
    )
```

```python
import functools

import jax
import jax.numpy as jnp
from jax import lax
from jax.experimental import pallas as pl
from jax.experimental.pallas import tpu as pltpu
from jax.sharding import PartitionSpec as P

TILE = 128
CURRENT = 2
STEP_SIZE = 1.0
PRIOR_PRECISION = 0.05
ARRIVALS = 4
GROUP = 3
LEVELS = 32767.0
TINY = 1e-30
MESH = pl.DeviceIdType.MESH
F32, BF16 = jnp.float32, jnp.bfloat16


def round_kernel(
    groups,
    width,
    choice_in,
    slots_in,
    positions_in,
    ancestors_in,
    design_in,
    labels_in,
    sections_in,
    advanced_out,
    mean_out,
    choice,
    slots,
    slots_wide,
    inverse_wide,
    inverse,
    positions,
    ancestors,
    labels,
    sections,
    advanced,
    gradient,
    design,
    narrow,
    picked,
    picked_all,
    lineage,
    resampled,
    outgoing,
    fetched,
    residual,
    terms,
    sums,
    incoming,
    peaks,
    peaks_in,
    outgoing_new,
    fetched_new,
    totals_own,
    totals_all,
    load_sem,
    inverse_sem,
    store_sem,
    dom_send,
    dom_recv,
    pos_send,
    pos_recv,
    out_send,
    out_recv,
    grad_send,
    grad_recv,
    peak_send,
    peak_recv,
    new_send,
    new_recv,
    tot_send,
    tot_recv,
):
    me, group = lax.axis_index("dp"), lax.axis_index("dom")
    particles = positions.shape[0]
    blocks_owned = positions.shape[1] // TILE
    per_block, blocks_dev = slots.shape
    loads = [
        pltpu.make_async_copy(source, target, load_sem.at[number])
        for number, (source, target) in enumerate(
            (
                (positions_in, positions),
                (choice_in, choice),
                (slots_in, slots_wide),
                (ancestors_in, ancestors),
                (slots_in, slots),
                (labels_in, labels),
                (sections_in, sections),
                (design_in, design),
            )
        )
    ]
    for load in loads:
        load.start()

    def to_dp(source, target, sends, receives, device):
        return pltpu.make_async_remote_copy(
            src_ref=source,
            dst_ref=target.at[me],
            send_sem=sends.at[device],
            recv_sem=receives.at[me],
            device_id=(group, device),
            device_id_type=MESH,
        )

    def from_dp(source, target, sends, receives, device):
        return pltpu.make_async_remote_copy(
            src_ref=source,
            dst_ref=target.at[device],
            send_sem=sends.at[device],
            recv_sem=receives.at[device],
            device_id=(group, device),
            device_id_type=MESH,
        )

    def others(body):
        def step(offset, carry):
            body(lax.rem(me + offset, width))
            return carry

        lax.fori_loop(1, width, step, 0)

    def grouped(body):
        size = GROUP if (width - 1) % GROUP == 0 else 1

        def step(turn, carry):
            body([lax.rem(me + 1 + turn * size + place, width) for place in range(size)])
            return carry

        lax.fori_loop(0, (width - 1) // size, step, 0)

    barrier = pltpu.get_barrier_semaphore()

    def greet(device):
        pl.semaphore_signal(barrier, inc=1, device_id=(group, device), device_id_type=MESH)

    others(greet)
    for offset in range(1, groups):
        pl.semaphore_signal(
            barrier, inc=1, device_id=(lax.rem(group + offset, groups), me), device_id_type=MESH
        )
    for load in loads[:4]:
        load.wait()
    for block in range(blocks_owned):
        narrow[block] = positions[:, block * TILE : (block + 1) * TILE].astype(BF16)

    def pick(device, carry):
        value = narrow[choice[device, me]]
        picked[device] = value
        picked_all[group, device] = value
        return carry

    lax.fori_loop(0, width, pick, 0)
    origin = lax.broadcasted_iota(jnp.int32, (groups * particles, particles), 0)
    hot = (origin == ancestors[...]).astype(F32).T.astype(BF16)
    tiles_dev = blocks_dev * per_block
    owner = lax.broadcasted_iota(jnp.int32, (width, blocks_dev), 0)
    first = lax.broadcasted_iota(jnp.int32, (width, blocks_dev), 1) * per_block
    found = jnp.full((width, blocks_dev), tiles_dev, jnp.int32)
    for place in range(per_block):
        found = jnp.where(slots_wide[place : place + 1, :] == owner, first + place, found)
    inverse_wide[...] = found
    inverse_copy = pltpu.make_async_copy(inverse_wide, inverse, inverse_sem)
    inverse_copy.start()
    pl.semaphore_wait(barrier, width + groups - 2)

    def dom_copy(device, offset, incoming_side):
        sign = groups - offset if incoming_side else offset
        peer = lax.rem(group + sign, groups)
        return pltpu.make_async_remote_copy(
            src_ref=picked.at[device],
            dst_ref=picked_all.at[peer if incoming_side else group, device],
            send_sem=dom_send.at[offset - 1, device],
            recv_sem=dom_recv.at[offset - 1, device],
            device_id=(peer, me),
            device_id_type=MESH,
        )

    def position_copy(offset, incoming_side):
        sign = groups - offset if incoming_side else offset
        peer = lax.rem(group + sign, groups)
        return pltpu.make_async_remote_copy(
            src_ref=positions,
            dst_ref=lineage.at[peer if incoming_side else group],
            send_sem=pos_send.at[offset - 1],
            recv_sem=pos_recv.at[offset - 1],
            device_id=(peer, me),
            device_id_type=MESH,
        )

    def send_picked(device):
        for offset in range(1, groups):
            dom_copy(device, offset, False).start()

    others(send_picked)
    send_picked(me)

    def resample(devices):
        for device in devices:
            for offset in range(1, groups):
                dom_copy(device, offset, True).wait_recv()
        rows = jnp.concatenate(
            [picked_all[:, device].reshape(groups * particles, TILE) for device in devices], axis=1
        )
        drawn = jnp.dot(hot, rows, preferred_element_type=F32).astype(BF16)
        return [drawn[:, place * TILE : (place + 1) * TILE] for place in range(len(devices))]

    def send_resampled(devices):
        for device, value in zip(devices, resample(devices)):
            outgoing[device] = value
        for device in devices:
            to_dp(outgoing.at[device], fetched, out_send, out_recv, device).start()

    grouped(send_resampled)
    fetched[me] = resample([me])[0]
    for offset in range(1, groups):
        position_copy(offset, False).start()
    terms[tiles_dev] = jnp.zeros((particles, TILE), F32)
    for load in loads[4:]:
        load.wait()
    inverse_copy.wait()
    others(lambda device: from_dp(outgoing.at[device], fetched, out_send, out_recv, device).wait_recv())

    def logits_of(source, row_block):
        weights = jnp.concatenate(
            [source[slots[place, row_block]] for place in range(per_block)], axis=1
        )
        tiles = design[pl.ds(pl.multiple_of(row_block * TILE, TILE), TILE), :]
        logits = lax.dot_general(
            tiles, weights, (((1,), (1,)), ((), ())), preferred_element_type=F32
        ).T
        target = labels[pl.ds(row_block, 1), :].astype(F32)
        section = sections[pl.ds(row_block, 1), :]
        return logits, target, section

    def residuals(row_block, carry):
        logits, target, section = logits_of(fetched, row_block)
        residual[row_block] = jnp.where(
            section <= CURRENT, target - jax.nn.sigmoid(logits), 0.0
        ).astype(BF16)
        return carry

    lax.fori_loop(0, blocks_dev, residuals, 0, unroll=8)

    def gradient_terms(row_block, carry):
        tiles = design[pl.ds(pl.multiple_of(row_block * TILE, TILE), TILE), :]
        product = jnp.dot(residual[row_block], tiles, preferred_element_type=F32)
        for place in range(per_block):
            terms[row_block * per_block + place] = product[:, place * TILE : (place + 1) * TILE]
        return carry

    lax.fori_loop(0, blocks_dev, gradient_terms, 0, unroll=8)

    def summed(device):
        total = terms[inverse[device, 0]]
        for row_block in range(1, blocks_dev):
            total = total + terms[inverse[device, row_block]]
        return total

    def send_sums(devices):
        for device in devices:
            total = summed(device)
            peak = jnp.max(jnp.abs(total), axis=0, keepdims=True)
            peaks[device] = peak
            coded = jnp.round(total * (LEVELS / jnp.maximum(peak, TINY)))
            sums[device] = coded.astype(jnp.int32).astype(jnp.int16)
        for device in devices:
            to_dp(peaks.at[device], peaks_in, peak_send, peak_recv, device).start()
            to_dp(sums.at[device], incoming, grad_send, grad_recv, device).start()

    grouped(send_sums)
    own = summed(me)
    own_choice = choice[me, me]
    for block in range(blocks_owned):
        gradient[block] = (own_choice == block).astype(F32) * own

    lineage[group] = positions[...]
    for offset in range(1, groups):
        position_copy(offset, True).wait_recv()
    for block in range(blocks_owned):
        span = slice(block * TILE, (block + 1) * TILE)
        rows = lineage[:, :, span].reshape(groups * particles, TILE)
        high = rows.astype(BF16)
        low = (rows - high.astype(F32)).astype(BF16)
        resampled[block] = jnp.dot(hot, high, preferred_element_type=F32) + jnp.dot(
            hot, low, preferred_element_type=F32
        )

    for start in range(1, width, ARRIVALS):
        devices = [
            lax.rem(me + offset, width) for offset in range(start, min(start + ARRIVALS, width))
        ]
        for device in devices:
            from_dp(peaks.at[device], peaks_in, peak_send, peak_recv, device).wait_recv()
            from_dp(sums.at[device], incoming, grad_send, grad_recv, device).wait_recv()
        arrived = [
            (
                choice[device, me],
                incoming[device].astype(jnp.int32).astype(F32)
                * (jnp.maximum(peaks_in[device], TINY) * (1.0 / LEVELS)),
            )
            for device in devices
        ]
        for block in range(blocks_owned):
            total = gradient[block]
            for chosen, value in arrived:
                total = total + (chosen == block).astype(F32) * value
            gradient[block] = total
    for block in range(blocks_owned):
        kept = resampled[block]
        moved = kept + STEP_SIZE * (gradient[block] - PRIOR_PRECISION * kept)
        advanced[:, block * TILE : (block + 1) * TILE] = moved
        narrow[block] = moved.astype(BF16)

    def send_new(devices):
        for device in devices:
            outgoing_new[device] = narrow[choice[device, me]]
        for device in devices:
            to_dp(outgoing_new.at[device], fetched_new, new_send, new_recv, device).start()

    grouped(send_new)
    store = pltpu.make_async_copy(advanced, advanced_out, store_sem)
    store.start()
    fetched_new[me] = narrow[choice[me, me]]
    others(
        lambda device: from_dp(
            outgoing_new.at[device], fetched_new, new_send, new_recv, device
        ).wait_recv()
    )

    def likelihood(row_block, carry):
        total, counted = carry
        logits, target, section = logits_of(fetched_new, row_block)
        chosen = section == CURRENT + 1
        softplus = jnp.maximum(logits, 0.0) + jnp.log(1.0 + jnp.exp(-jnp.abs(logits)))
        return (
            total + jnp.where(chosen, target * logits - softplus, 0.0),
            counted + chosen.astype(F32),
        )

    total, counted = lax.fori_loop(
        0,
        blocks_dev,
        likelihood,
        (jnp.zeros((particles, TILE), F32), jnp.zeros((1, TILE), F32)),
        unroll=8,
    )
    both = jnp.concatenate([total, jnp.broadcast_to(counted, (particles, TILE))], axis=0)
    row = jnp.sum(both.T, axis=0, keepdims=True)
    row = jnp.broadcast_to(row, totals_own.shape)
    totals_own[...] = row
    totals_all[me] = row
    others(lambda device: to_dp(totals_own, totals_all, tot_send, tot_recv, device).start())
    others(lambda device: from_dp(totals_own, totals_all, tot_send, tot_recv, device).wait_recv())
    final = jnp.sum(totals_all[...], axis=0)
    mean_out[...] = final[:1, :particles] / jnp.maximum(final[:1, particles:], 1.0)

    def wait_sends(device):
        to_dp(outgoing.at[device], fetched, out_send, out_recv, device).wait_send()
        to_dp(sums.at[device], incoming, grad_send, grad_recv, device).wait_send()
        to_dp(peaks.at[device], peaks_in, peak_send, peak_recv, device).wait_send()
        to_dp(outgoing_new.at[device], fetched_new, new_send, new_recv, device).wait_send()
        to_dp(totals_own, totals_all, tot_send, tot_recv, device).wait_send()

    others(wait_sends)
    store.wait()

    def wait_dom(device, carry):
        for offset in range(1, groups):
            dom_copy(device, offset, False).wait_send()
        return carry

    lax.fori_loop(0, width, wait_dom, 0)
    for offset in range(1, groups):
        position_copy(offset, False).wait_send()


def shards(positions, ancestors, block_choice, tile_slot, design, labels, row_section):
    width, groups = lax.axis_size("dp"), lax.axis_size("dom")
    particles, features = positions.shape
    blocks_owned = features // TILE
    blocks_dev, per_block = tile_slot.shape
    tiles = blocks_dev * per_block

    hbm = pl.BlockSpec(memory_space=pl.ANY)
    vmem = pl.BlockSpec(memory_space=pltpu.VMEM)
    block = (particles, TILE)
    dma = pltpu.SemaphoreType.DMA
    advanced, mean = pl.pallas_call(
        functools.partial(round_kernel, groups, width),
        out_shape=(
            jax.ShapeDtypeStruct((particles, features), F32),
            jax.ShapeDtypeStruct((1, particles), F32),
        ),
        in_specs=[hbm] * 7,
        out_specs=(hbm, vmem),
        scratch_shapes=[
            pltpu.SMEM((width, width), jnp.int32),
            pltpu.SMEM((per_block, blocks_dev), jnp.int32),
            pltpu.VMEM((per_block, blocks_dev), jnp.int32),
            pltpu.VMEM((width, blocks_dev), jnp.int32),
            pltpu.SMEM((width, blocks_dev), jnp.int32),
            pltpu.VMEM((particles, features), F32),
            pltpu.VMEM((1, particles), jnp.int32),
            pltpu.VMEM((blocks_dev, TILE), jnp.int32),
            pltpu.VMEM((blocks_dev, TILE), jnp.int32),
            pltpu.VMEM((particles, features), F32),
            pltpu.VMEM((blocks_owned, *block), F32),
            pltpu.VMEM(design.shape, BF16),
            pltpu.VMEM((blocks_owned, *block), BF16),
            pltpu.VMEM((width, *block), BF16),
            pltpu.VMEM((groups, width, *block), BF16),
            pltpu.VMEM((groups, particles, features), F32),
            pltpu.VMEM((blocks_owned, *block), F32),
            pltpu.VMEM((width, *block), BF16),
            pltpu.VMEM((width, *block), BF16),
            pltpu.VMEM((blocks_dev, *block), BF16),
            pltpu.VMEM((tiles + 1, *block), F32),
            pltpu.VMEM((width, *block), jnp.int16),
            pltpu.VMEM((width, *block), jnp.int16),
            pltpu.VMEM((width, 1, TILE), F32),
            pltpu.VMEM((width, 1, TILE), F32),
            pltpu.VMEM((width, *block), BF16),
            pltpu.VMEM((width, *block), BF16),
            pltpu.VMEM((8, 2 * particles), F32),
            pltpu.VMEM((width, 8, 2 * particles), F32),
            dma((8,)),
            dma,
            dma,
            dma((max(groups - 1, 1), width)),
            dma((max(groups - 1, 1), width)),
            dma((max(groups - 1, 1),)),
            dma((max(groups - 1, 1),)),
            dma((width,)),
            dma((width,)),
            dma((width,)),
            dma((width,)),
            dma((width,)),
            dma((width,)),
            dma((width,)),
            dma((width,)),
            dma((width,)),
            dma((width,)),
        ],
        compiler_params=pltpu.CompilerParams(
            collective_id=0, has_side_effects=True, vmem_limit_bytes=60 << 20
        ),
        name="smc_round",
    )(
        block_choice,
        tile_slot.T,
        positions,
        ancestors.reshape(1, particles),
        design,
        labels.reshape(blocks_dev, TILE),
        row_section.reshape(blocks_dev, TILE),
    )
    return advanced, mean.reshape(particles)


def solution(mesh):
    return jax.shard_map(
        shards,
        mesh=mesh,
        in_specs=(P("dom", "dp"), P("dom"), P(), P("dp", None), P("dp", None), P("dp"), P("dp")),
        out_specs=(P("dom", "dp"), P("dom")),
        check_vma=False,
    )
```

```python
import functools

import jax
import jax.numpy as jnp
from jax import lax
from jax.experimental import pallas as pl
from jax.experimental.pallas import tpu as pltpu
from jax.sharding import PartitionSpec as P

TILE = 128
CURRENT = 2
STEP_SIZE = 1.0
PRIOR_PRECISION = 0.05
ARRIVALS = 4
LEVELS = 32767.0
TINY = 1e-30
MESH = pl.DeviceIdType.MESH
F32, BF16 = jnp.float32, jnp.bfloat16


def round_kernel(
    groups,
    width,
    choice_in,
    slots_in,
    positions_in,
    ancestors_in,
    design_in,
    labels_in,
    sections_in,
    advanced_out,
    mean_out,
    choice,
    slots,
    slots_wide,
    inverse_wide,
    inverse,
    positions,
    ancestors,
    labels,
    sections,
    advanced,
    gradient,
    design,
    narrow,
    picked,
    picked_all,
    coded_peak,
    coded_rows,
    lineage_peak,
    lineage_rows,
    lineage,
    resampled,
    outgoing,
    fetched,
    residual,
    terms,
    sums,
    incoming,
    peaks,
    peaks_in,
    outgoing_new,
    fetched_new,
    totals_own,
    totals_all,
    load_sem,
    inverse_sem,
    store_sem,
    dom_send,
    dom_recv,
    pos_send,
    pos_recv,
    out_send,
    out_recv,
    grad_send,
    grad_recv,
    peak_send,
    peak_recv,
    new_send,
    new_recv,
    tot_send,
    tot_recv,
):
    me, group = lax.axis_index("dp"), lax.axis_index("dom")
    particles = positions.shape[0]
    blocks_owned = positions.shape[1] // TILE
    per_block, blocks_dev = slots.shape
    loads = [
        pltpu.make_async_copy(source, target, load_sem.at[number])
        for number, (source, target) in enumerate(
            (
                (positions_in, positions),
                (choice_in, choice),
                (slots_in, slots_wide),
                (ancestors_in, ancestors),
                (slots_in, slots),
                (labels_in, labels),
                (sections_in, sections),
                (design_in, design),
            )
        )
    ]
    for load in loads:
        load.start()

    def to_dp(source, target, sends, receives, device):
        return pltpu.make_async_remote_copy(
            src_ref=source,
            dst_ref=target.at[me],
            send_sem=sends.at[device],
            recv_sem=receives.at[me],
            device_id=(group, device),
            device_id_type=MESH,
        )

    def from_dp(source, target, sends, receives, device):
        return pltpu.make_async_remote_copy(
            src_ref=source,
            dst_ref=target.at[device],
            send_sem=sends.at[device],
            recv_sem=receives.at[device],
            device_id=(group, device),
            device_id_type=MESH,
        )

    def others(body):
        def step(offset, carry):
            body(lax.rem(me + offset, width))
            return carry

        lax.fori_loop(1, width, step, 0)

    barrier = pltpu.get_barrier_semaphore()

    def greet(device):
        pl.semaphore_signal(barrier, inc=1, device_id=(group, device), device_id_type=MESH)

    others(greet)
    for offset in range(1, groups):
        pl.semaphore_signal(
            barrier, inc=1, device_id=(lax.rem(group + offset, groups), me), device_id_type=MESH
        )
    for load in loads[:4]:
        load.wait()
    for block in range(blocks_owned):
        narrow[block] = positions[:, block * TILE : (block + 1) * TILE].astype(BF16)

    def pick(device, carry):
        value = narrow[choice[device, me]]
        picked[device] = value
        picked_all[group, device] = value
        return carry

    lax.fori_loop(0, width, pick, 0)
    origin = lax.broadcasted_iota(jnp.int32, (groups * particles, particles), 0)
    hot = (origin == ancestors[...]).astype(F32).T.astype(BF16)
    tiles_dev = blocks_dev * per_block
    owner = lax.broadcasted_iota(jnp.int32, (width, blocks_dev), 0)
    first = lax.broadcasted_iota(jnp.int32, (width, blocks_dev), 1) * per_block
    found = jnp.full((width, blocks_dev), tiles_dev, jnp.int32)
    for place in range(per_block):
        found = jnp.where(slots_wide[place : place + 1, :] == owner, first + place, found)
    inverse_wide[...] = found
    inverse_copy = pltpu.make_async_copy(inverse_wide, inverse, inverse_sem)
    inverse_copy.start()
    pl.semaphore_wait(barrier, width + groups - 2)

    def dom_copy(device, offset, incoming_side):
        sign = groups - offset if incoming_side else offset
        peer = lax.rem(group + sign, groups)
        return pltpu.make_async_remote_copy(
            src_ref=picked.at[device],
            dst_ref=picked_all.at[peer if incoming_side else group, device],
            send_sem=dom_send.at[offset - 1, device],
            recv_sem=dom_recv.at[offset - 1, device],
            device_id=(peer, me),
            device_id_type=MESH,
        )

    def position_copies(offset, incoming_side):
        sign = groups - offset if incoming_side else offset
        peer = lax.rem(group + sign, groups)
        return [
            pltpu.make_async_remote_copy(
                src_ref=source,
                dst_ref=target.at[peer if incoming_side else group],
                send_sem=pos_send.at[kind, offset - 1],
                recv_sem=pos_recv.at[kind, offset - 1],
                device_id=(peer, me),
                device_id_type=MESH,
            )
            for kind, (source, target) in enumerate(
                ((coded_peak, lineage_peak), (coded_rows, lineage_rows))
            )
        ]

    def send_picked(device):
        for offset in range(1, groups):
            dom_copy(device, offset, False).start()

    others(send_picked)
    send_picked(me)

    def resample(device):
        for offset in range(1, groups):
            dom_copy(device, offset, True).wait_recv()
        rows = picked_all[:, device].reshape(groups * particles, TILE)
        return jnp.dot(hot, rows, preferred_element_type=F32).astype(BF16)

    def send_resampled(device):
        outgoing[device] = resample(device)
        to_dp(outgoing.at[device], fetched, out_send, out_recv, device).start()

    others(send_resampled)
    fetched[me] = resample(me)
    own_peak = jnp.max(jnp.abs(positions[...]), axis=0, keepdims=True)
    coded_peak[...] = own_peak
    coded_rows[...] = (
        jnp.round(positions[...] * (LEVELS / jnp.maximum(own_peak, TINY)))
        .astype(jnp.int32)
        .astype(jnp.int16)
    )
    for offset in range(1, groups):
        for copy in position_copies(offset, False):
            copy.start()
    terms[tiles_dev] = jnp.zeros((particles, TILE), F32)
    for load in loads[4:]:
        load.wait()
    inverse_copy.wait()
    others(lambda device: from_dp(outgoing.at[device], fetched, out_send, out_recv, device).wait_recv())

    def logits_of(source, row_block):
        weights = jnp.concatenate(
            [source[slots[place, row_block]] for place in range(per_block)], axis=1
        )
        tiles = design[pl.ds(pl.multiple_of(row_block * TILE, TILE), TILE), :]
        logits = lax.dot_general(
            weights, tiles, (((1,), (1,)), ((), ())), preferred_element_type=F32
        )
        target = labels[pl.ds(row_block, 1), :].astype(F32)
        section = sections[pl.ds(row_block, 1), :]
        return logits, target, section

    def residuals(row_block, carry):
        logits, target, section = logits_of(fetched, row_block)
        residual[row_block] = jnp.where(
            section <= CURRENT, target - jax.nn.sigmoid(logits), 0.0
        ).astype(BF16)
        return carry

    lax.fori_loop(0, blocks_dev, residuals, 0, unroll=8)

    def gradient_terms(row_block, carry):
        tiles = design[pl.ds(pl.multiple_of(row_block * TILE, TILE), TILE), :]
        product = jnp.dot(residual[row_block], tiles, preferred_element_type=F32)
        for place in range(per_block):
            terms[row_block * per_block + place] = product[:, place * TILE : (place + 1) * TILE]
        return carry

    lax.fori_loop(0, blocks_dev, gradient_terms, 0, unroll=8)

    def summed(device):
        total = terms[inverse[device, 0]]
        for row_block in range(1, blocks_dev):
            total = total + terms[inverse[device, row_block]]
        return total

    def send_sum(device):
        total = summed(device)
        peak = jnp.max(jnp.abs(total), axis=0, keepdims=True)
        peaks[device] = peak
        to_dp(peaks.at[device], peaks_in, peak_send, peak_recv, device).start()
        coded = jnp.round(total * (LEVELS / jnp.maximum(peak, TINY)))
        sums[device] = coded.astype(jnp.int32).astype(jnp.int16)
        to_dp(sums.at[device], incoming, grad_send, grad_recv, device).start()

    others(send_sum)
    own = summed(me)
    own_choice = choice[me, me]
    for block in range(blocks_owned):
        gradient[block] = (own_choice == block).astype(F32) * own

    lineage[group] = positions[...]
    for offset in range(1, groups):
        for copy in position_copies(offset, True):
            copy.wait_recv()
        peer = lax.rem(group + groups - offset, groups)
        lineage[peer] = lineage_rows[peer].astype(jnp.int32).astype(F32) * (
            jnp.maximum(lineage_peak[peer], TINY) * (1.0 / LEVELS)
        )
    for block in range(blocks_owned):
        span = slice(block * TILE, (block + 1) * TILE)
        rows = lineage[:, :, span].reshape(groups * particles, TILE)
        high = rows.astype(BF16)
        low = (rows - high.astype(F32)).astype(BF16)
        resampled[block] = jnp.dot(hot, high, preferred_element_type=F32) + jnp.dot(
            hot, low, preferred_element_type=F32
        )

    for start in range(1, width, ARRIVALS):
        devices = [
            lax.rem(me + offset, width) for offset in range(start, min(start + ARRIVALS, width))
        ]
        for device in devices:
            from_dp(peaks.at[device], peaks_in, peak_send, peak_recv, device).wait_recv()
            from_dp(sums.at[device], incoming, grad_send, grad_recv, device).wait_recv()
        arrived = [
            (
                choice[device, me],
                incoming[device].astype(jnp.int32).astype(F32)
                * (jnp.maximum(peaks_in[device], TINY) * (1.0 / LEVELS)),
            )
            for device in devices
        ]
        for block in range(blocks_owned):
            total = gradient[block]
            for chosen, value in arrived:
                total = total + (chosen == block).astype(F32) * value
            gradient[block] = total
    for block in range(blocks_owned):
        kept = resampled[block]
        moved = kept + STEP_SIZE * (gradient[block] - PRIOR_PRECISION * kept)
        advanced[:, block * TILE : (block + 1) * TILE] = moved
        narrow[block] = moved.astype(BF16)

    def send_new(device):
        outgoing_new[device] = narrow[choice[device, me]]
        to_dp(outgoing_new.at[device], fetched_new, new_send, new_recv, device).start()

    others(send_new)
    store = pltpu.make_async_copy(advanced, advanced_out, store_sem)
    store.start()
    fetched_new[me] = narrow[choice[me, me]]
    others(
        lambda device: from_dp(
            outgoing_new.at[device], fetched_new, new_send, new_recv, device
        ).wait_recv()
    )

    def likelihood(row_block, carry):
        total, counted = carry
        logits, target, section = logits_of(fetched_new, row_block)
        chosen = section == CURRENT + 1
        softplus = jnp.maximum(logits, 0.0) + jnp.log(1.0 + jnp.exp(-jnp.abs(logits)))
        return (
            total + jnp.where(chosen, target * logits - softplus, 0.0),
            counted + chosen.astype(F32),
        )

    total, counted = lax.fori_loop(
        0,
        blocks_dev,
        likelihood,
        (jnp.zeros((particles, TILE), F32), jnp.zeros((1, TILE), F32)),
        unroll=8,
    )
    both = jnp.concatenate([total, jnp.broadcast_to(counted, (particles, TILE))], axis=0)
    row = jnp.sum(both.T, axis=0, keepdims=True)
    row = jnp.broadcast_to(row, totals_own.shape)
    totals_own[...] = row
    totals_all[me] = row
    others(lambda device: to_dp(totals_own, totals_all, tot_send, tot_recv, device).start())
    others(lambda device: from_dp(totals_own, totals_all, tot_send, tot_recv, device).wait_recv())
    final = jnp.sum(totals_all[...], axis=0)
    mean_out[...] = final[:1, :particles] / jnp.maximum(final[:1, particles:], 1.0)

    def wait_sends(device):
        to_dp(outgoing.at[device], fetched, out_send, out_recv, device).wait_send()
        to_dp(sums.at[device], incoming, grad_send, grad_recv, device).wait_send()
        to_dp(peaks.at[device], peaks_in, peak_send, peak_recv, device).wait_send()
        to_dp(outgoing_new.at[device], fetched_new, new_send, new_recv, device).wait_send()
        to_dp(totals_own, totals_all, tot_send, tot_recv, device).wait_send()

    others(wait_sends)
    store.wait()

    def wait_dom(device, carry):
        for offset in range(1, groups):
            dom_copy(device, offset, False).wait_send()
        return carry

    lax.fori_loop(0, width, wait_dom, 0)
    for offset in range(1, groups):
        for copy in position_copies(offset, False):
            copy.wait_send()


def shards(positions, ancestors, block_choice, tile_slot, design, labels, row_section):
    width, groups = lax.axis_size("dp"), lax.axis_size("dom")
    particles, features = positions.shape
    blocks_owned = features // TILE
    blocks_dev, per_block = tile_slot.shape
    tiles = blocks_dev * per_block

    hbm = pl.BlockSpec(memory_space=pl.ANY)
    vmem = pl.BlockSpec(memory_space=pltpu.VMEM)
    block = (particles, TILE)
    dma = pltpu.SemaphoreType.DMA
    advanced, mean = pl.pallas_call(
        functools.partial(round_kernel, groups, width),
        out_shape=(
            jax.ShapeDtypeStruct((particles, features), F32),
            jax.ShapeDtypeStruct((1, particles), F32),
        ),
        in_specs=[hbm] * 7,
        out_specs=(hbm, vmem),
        scratch_shapes=[
            pltpu.SMEM((width, width), jnp.int32),
            pltpu.SMEM((per_block, blocks_dev), jnp.int32),
            pltpu.VMEM((per_block, blocks_dev), jnp.int32),
            pltpu.VMEM((width, blocks_dev), jnp.int32),
            pltpu.SMEM((width, blocks_dev), jnp.int32),
            pltpu.VMEM((particles, features), F32),
            pltpu.VMEM((1, particles), jnp.int32),
            pltpu.VMEM((blocks_dev, TILE), jnp.int32),
            pltpu.VMEM((blocks_dev, TILE), jnp.int32),
            pltpu.VMEM((particles, features), F32),
            pltpu.VMEM((blocks_owned, *block), F32),
            pltpu.VMEM(design.shape, BF16),
            pltpu.VMEM((blocks_owned, *block), BF16),
            pltpu.VMEM((width, *block), BF16),
            pltpu.VMEM((groups, width, *block), BF16),
            pltpu.VMEM((1, features), F32),
            pltpu.VMEM((particles, features), jnp.int16),
            pltpu.VMEM((groups, 1, features), F32),
            pltpu.VMEM((groups, particles, features), jnp.int16),
            pltpu.VMEM((groups, particles, features), F32),
            pltpu.VMEM((blocks_owned, *block), F32),
            pltpu.VMEM((width, *block), BF16),
            pltpu.VMEM((width, *block), BF16),
            pltpu.VMEM((blocks_dev, *block), BF16),
            pltpu.VMEM((tiles + 1, *block), F32),
            pltpu.VMEM((width, *block), jnp.int16),
            pltpu.VMEM((width, *block), jnp.int16),
            pltpu.VMEM((width, 1, TILE), F32),
            pltpu.VMEM((width, 1, TILE), F32),
            pltpu.VMEM((width, *block), BF16),
            pltpu.VMEM((width, *block), BF16),
            pltpu.VMEM((8, 2 * particles), F32),
            pltpu.VMEM((width, 8, 2 * particles), F32),
            dma((8,)),
            dma,
            dma,
            dma((max(groups - 1, 1), width)),
            dma((max(groups - 1, 1), width)),
            dma((2, max(groups - 1, 1))),
            dma((2, max(groups - 1, 1))),
            dma((width,)),
            dma((width,)),
            dma((width,)),
            dma((width,)),
            dma((width,)),
            dma((width,)),
            dma((width,)),
            dma((width,)),
            dma((width,)),
            dma((width,)),
        ],
        compiler_params=pltpu.CompilerParams(
            collective_id=0, has_side_effects=True, vmem_limit_bytes=60 << 20
        ),
        name="smc_round",
    )(
        block_choice,
        tile_slot.T,
        positions,
        ancestors.reshape(1, particles),
        design,
        labels.reshape(blocks_dev, TILE),
        row_section.reshape(blocks_dev, TILE),
    )
    return advanced, mean.reshape(particles)


def solution(mesh):
    return jax.shard_map(
        shards,
        mesh=mesh,
        in_specs=(P("dom", "dp"), P("dom"), P(), P("dp", None), P("dp", None), P("dp"), P("dp")),
        out_specs=(P("dom", "dp"), P("dom")),
        check_vma=False,
    )
```
